128 devices in a mesh: dp: 16 (over y, z), fsdp: 8 (over x, core).
Axes of the slice: x: 4, y: 4, z: 4, core: 2. Of those that a mesh axis runs over, the one named last changes fastest.
Arguments:
- ctx: bfloat16 [16384, 4096], P(('dp', 'fsdp')), may hold values from -0.5 to 0.5
- grad_out: bfloat16 [16384, 4096], P(('dp', 'fsdp')), may hold values from -6 to 6
- weight: bfloat16 [4096, 4096], P(None, 'fsdp'), may hold values from -0.09375 to 0.09375
- error: float32 [16, 4096, 4096], P('dp', 'fsdp'), may hold values from -6 to 6
- q_init: float32 [4096, 64], P('fsdp'), may hold values from -2 to 3
Outputs:
- grad_ctx: bfloat16 [16384, 4096], P(('dp', 'fsdp'))
- q_factor: float32 [4096, 64], P('fsdp')
- new_error: float32 [16, 4096, 4096], P('dp', 'fsdp')
The draws below stay inside these ranges and needn't reach their ends.
All inputs are finite; a program needn't handle non-finite values.
Results may differ from the reference program's by a relative error of at most 0.0007.
Values may be sent and summed in bfloat16 or wider, within the bound.
No kernel may reach another device: no remote copies, remote signals or barrier semaphores. Data moves between devices by JAX's collectives and lax.ppermute only.
A program may use at most 128 MiB of HBM per device.

```python
import jax
import jax.numpy as jnp
from jax import lax

D = 4096
RANK = 64
TOK_DEV = 128
INNER = 4096
REPLICA_TOK = 1024
TOKENS = 16384
N_DP = 16
N_FSDP = 8


def draw_error(key, part):
    key = jax.random.fold_in(key, 11)
    first = jax.random.fold_in(key, 0)
    return jnp.clip(jax.random.normal(first, (N_DP, D, INNER), jnp.float32), -6.0, 6.0)


def draw_q_init(key, part):
    key = jax.random.fold_in(key, 23)
    rows = jnp.arange(D, dtype=jnp.int32)[:, None]
    cols = jnp.arange(RANK, dtype=jnp.int32)[None, :]
    pattern = jnp.where(rows % RANK == cols, 1.0, 0.0).astype(jnp.float32)
    noise = jnp.clip(0.5 * jax.random.normal(key, (D, RANK), jnp.float32), -1.5, 1.5)
    return pattern + noise


def steps_of(key, extent, shards, smallest, high):
    gain = 1.0
    for position, shards_of in shards:
        steps = jax.random.uniform(jax.random.fold_in(jax.random.fold_in(key, 6), position), (shards_of,), jnp.float32, smallest / len(shards), high / len(shards))
        gain = gain * jnp.repeat(jnp.exp(steps), extent[position] // shards_of).reshape((-1,) + (1,) * (len(extent) - 1 - position))
    return gain


def bell_draw(rng, extent, scale, bound, pieces=(), held_as=jnp.bfloat16):
    result = jax.random.normal(rng, extent, jnp.float32) * scale
    if len(pieces) > 0:
        result = steps_of(rng, extent, pieces, -0.22, 0.18) * result
    return jnp.clip(result, min=-bound, max=bound).astype(held_as)


def setup_inputs(seed: int = 0) -> dict:
    key_of = jax.random.split(jax.random.key(seed), 6)
    ctx = bell_draw(key_of[0], (TOKENS, INNER), (REPLICA_TOK ** -0.5), 0.5, ((0, 128),))
    grad_out = bell_draw(key_of[1], (TOKENS, D), 1.0, 6.0, ((0, 128),))
    weight = bell_draw(key_of[2], (INNER, D), INNER ** -0.5, 0.09375, ((1, 8),))
    error = draw_error(jax.random.fold_in(key_of[5], 71), 0)
    q_init = draw_q_init(jax.random.fold_in(key_of[5], 71), 0)
    return {"ctx": ctx, "grad_out": grad_out, "weight": weight, "error": error, "q_init": q_init}


def orthonormal(p_raw):
    gram_matrix = jnp.dot(p_raw.T, p_raw, precision=lax.Precision.HIGHEST)
    factor_low = jnp.linalg.cholesky(gram_matrix)
    solved = jax.scipy.linalg.solve_triangular(factor_low, p_raw.T, lower=True)
    return solved.T

def reference(ctx, grad_out, weight, error, q_init):
    grad_ctx = jnp.dot(grad_out.astype(jnp.float32), weight.T.astype(jnp.float32), preferred_element_type=jnp.float32).astype(jnp.bfloat16)
    replica_rows = TOK_DEV * N_FSDP

    def replica_grad(replica):
        offset = (replica * replica_rows).astype(jnp.int32)
        ctx_part = lax.dynamic_slice_in_dim(ctx, offset, replica_rows, 0)
        out_part = lax.dynamic_slice_in_dim(grad_out, offset, replica_rows, 0)
        local_grad = lax.dot_general(out_part.astype(jnp.float32), ctx_part.astype(jnp.float32), (((0,), (0,)), ((), ())), preferred_element_type=jnp.float32)
        return local_grad + error[replica]
    merged = lax.map(replica_grad, jnp.arange(N_DP, dtype=jnp.int32))
    p_raw = jnp.einsum('kdi,dr->ir', merged, q_init, precision=lax.Precision.HIGHEST)
    p_factor = orthonormal(p_raw)
    q_factor = jnp.einsum('kdi,ir->dr', merged, p_factor, precision=lax.Precision.HIGHEST) / N_DP
    approx = jnp.dot(q_factor, p_factor.T, precision=lax.Precision.HIGHEST)
    new_error = merged - approx[None]
    return (grad_ctx, q_factor, new_error)
```

```python
import functools

import jax
import jax.numpy as jnp
from jax import lax
from jax.experimental import pallas as pl
from jax.experimental.pallas import tpu as pltpu
from jax.sharding import PartitionSpec as P

F32, BF16 = jnp.float32, jnp.bfloat16
VMEM = pl.BlockSpec(memory_space=pltpu.VMEM)
SMEM = pl.BlockSpec(memory_space=pltpu.SMEM)
HBM = pl.BlockSpec(memory_space=pltpu.HBM)
RELATIVE = [(a, d) for a in range(2) for d in range(4)]
NT = (((1,), (1,)), ((), ()))
NN = (((1,), (0,)), ((), ()))


def mm(lhs, rhs, dims=NN, precision=None):
    return lax.dot_general(lhs, rhs, dims, precision=precision, preferred_element_type=F32)


def halves(value):
    high = value.astype(BF16)
    return high, (value - high.astype(F32)).astype(BF16)


def thirds(value):
    high = value.astype(BF16)
    rest = value - high.astype(F32)
    mid = rest.astype(BF16)
    return high, mid, (rest - mid.astype(F32)).astype(BF16)


def along_x(value, d):
    return lax.ppermute(value, "fsdp", [(i, ((i // 2 + d) % 4) * 2 + i % 2) for i in range(8)])


def along_y(value, d):
    return lax.ppermute(value, "dp", [(i, ((i // 4 + d) % 4) * 4 + i % 4) for i in range(16)])


def along_z(value, d):
    return lax.ppermute(value, "dp", [(i, (i // 4) * 4 + (i % 4 + d) % 4) for i in range(16)])


def other_core(value):
    return lax.ppermute(value, "fsdp", [(i, i ^ 1) for i in range(8)])


def to_relative(value, a, d):
    return lax.ppermute(value, "fsdp", [(i, ((i // 2 + d) % 4) * 2 + (i % 2 ^ a)) for i in range(8)])


def pallas(body, out_shape, flops=0, bytes_accessed=0, mib=16, **kw):
    return pl.pallas_call(
        body,
        out_shape=out_shape,
        compiler_params=pltpu.CompilerParams(vmem_limit_bytes=mib * 2**20),
        cost_estimate=pl.CostEstimate(flops=int(flops), bytes_accessed=int(bytes_accessed), transcendentals=0),
        **kw,
    )


def in_hbm(value):
    return pltpu.with_memory_space_constraint(value, pltpu.HBM)


def shaped(shape, dtype=F32):
    return jax.ShapeDtypeStruct(shape, dtype)


def after(value, *earlier):
    return lax.optimization_barrier((value, *earlier))[0]


def chunk_of(x, c, a, d):
    return lax.rem(x + d, 4) * 2 + (c ^ a)


def rank_row(z, c, a, d):
    return pl.multiple_of((c ^ a) * 32 + lax.rem(z + d, 4) * 8, 8)


def cut_body(place, grad, *outs):
    x, c = place[0], place[1]
    for d, out in enumerate(outs):
        for a in range(2):
            out[a] = grad[:, pl.ds(pl.multiple_of(chunk_of(x, c, a, d) * 512, 512), 512)]


def cut(place, grad):
    return pallas(
        cut_body, [shaped((2, 128, 512), BF16)] * 4, bytes_accessed=2 << 20, in_specs=[SMEM, VMEM], out_specs=[VMEM] * 4
    )(place, grad)


def columns(i):
    return slice(512 * i, 512 * i + 512)


def fetch(source, held, arrived):
    copies = [pltpu.make_async_copy(source.at[:, columns(i)], held.at[:, columns(i)], arrived.at[i]) for i in range(8)]
    for copy in copies:
        copy.start()
    return copies


def error_left_body(place, qt, error, out, held, arrived, pieces):
    c, z = place[1], place[3]
    copies = fetch(error, held, arrived)
    for n, (a, d) in enumerate(RELATIVE):
        rows = qt[pl.ds(rank_row(z, c, a, d), 8), :]
        high = rows.astype(BF16).astype(F32)
        pieces[8 * n : 8 * n + 8, :] = high
        pieces[64 + 8 * n : 72 + 8 * n, :] = rows - high
    q = pieces[...].astype(BF16)
    for i, copy in enumerate(copies):
        copy.wait()
        high, low = halves(held[:, columns(i)])
        first = mm(q, high)
        out[:, columns(i)] = first[:64] + first[64:] + mm(q[:64], low)


def error_left(place, qt, error):
    return pallas(
        error_left_body,
        shaped((64, 4096)),
        flops=2 * 512 * 4096 * 192,
        bytes_accessed=9 << 20,
        in_specs=[SMEM, VMEM, HBM],
        out_specs=VMEM,
        scratch_shapes=[pltpu.VMEM((512, 4096), F32), pltpu.SemaphoreType.DMA((8,)), pltpu.VMEM((128, 512), F32)],
    )(place, qt, in_hbm(error))


def left_body(place, q0, q1, q2, q3, q_far, grad, ctx, term, near, far, g_abs, g_rel):
    x, c, z = place[0], place[1], place[3]
    total = jnp.zeros((64, 128), F32)
    for a, d in RELATIVE:
        q = (q0, q1, q2, q3)[d][...] if a == 0 else q_far[64 * d : 64 * d + 64, :]
        chunk = grad[:, pl.ds(pl.multiple_of(chunk_of(x, c, a, d) * 512, 512), 512)]
        parts = mm(jnp.concatenate(thirds(q), 0), chunk, NT)
        total += parts[:64] + parts[64:128] + parts[128:]
    g_abs[...] = total
    for n, (a, d) in enumerate(RELATIVE):
        g_rel[8 * n : 8 * n + 8, :] = g_abs[pl.ds(rank_row(z, c, a, d), 8), :]
    g = jnp.concatenate(thirds(g_rel[...]), 0)
    for i in range(4):
        at = slice(1024 * i, 1024 * i + 1024)
        parts = mm(g, ctx[:, at])
        whole = term[:, at] + (parts[:64] + parts[64:128] + parts[128:])
        near[:, at] = whole[:32]
        far[:, at] = whole[32:]


def left(place, q_near, q_far, grad, ctx, term):
    return pallas(
        left_body,
        [shaped((32, 4096))] * 2,
        flops=4 * 192 * 128 * 4096,
        bytes_accessed=5 << 20,
        in_specs=[SMEM] + [VMEM] * 8,
        out_specs=[VMEM] * 2,
        scratch_shapes=[pltpu.VMEM((64, 128), F32)] * 2,
    )(place, *q_near, q_far, grad, ctx, term)


def join_body(place, v0, v1, v2, v3, out):
    z = place[3]
    for d, value in enumerate((v0, v1, v2, v3)):
        out[:, pl.ds(pl.multiple_of(lax.rem(z + d, 4) * 1024, 1024), 1024)] = value[...]


def join(place, values):
    return pallas(
        join_body, shaped((values[0].shape[0], 4096), values[0].dtype), bytes_accessed=1 << 18, in_specs=[SMEM] + [VMEM] * 4, out_specs=VMEM
    )(place, *values)


def turn_body(place, c0, c1, c2, c3, c_far, out):
    x, c = place[0], place[1]
    for a, d in RELATIVE:
        chunk = (c0, c1, c2, c3)[d][0] if a == 0 else c_far[d]
        source = chunk_of(x, c, a, 4 - d)
        out[:, pl.ds(pl.multiple_of(source * 128, 128), 128)] = chunk.T


def turn(place, chunks, far):
    return pallas(
        turn_body, shaped((512, 1024), BF16), bytes_accessed=2 << 20, in_specs=[SMEM] + [VMEM] * 5, out_specs=VMEM
    )(place, *chunks, far)


def middle_body(place, p0, p1, p2, p3, p_far, ctx, p_out, u_out):
    c, z = place[1], place[3]
    for a, d in RELATIVE:
        p_out[pl.ds(rank_row(z, c, a, d), 8), :] = (p0, p1, p2, p3)[d][...] if a == 0 else p_far[8 * d : 8 * d + 8, :]
    u = jnp.zeros((64, 128), F32)
    for i in range(4):
        at = slice(1024 * i, 1024 * i + 1024)
        parts = mm(jnp.concatenate(thirds(p_out[:, at]), 0), ctx[:, at], NT)
        u += parts[:64] + parts[64:128] + parts[128:]
    u_out[...] = u


def middle(place, p_near, p_far, ctx):
    return pallas(
        middle_body,
        [shaped((64, 4096)), shaped((64, 128))],
        flops=2 * 192 * 128 * 4096,
        bytes_accessed=4 << 20,
        in_specs=[SMEM] + [VMEM] * 6,
        out_specs=[VMEM] * 2,
    )(place, *p_near, p_far, ctx)


def right_body(p_raw, error, out, held, arrived):
    for i, copy in enumerate(fetch(error, held, arrived)):
        high, low = halves(p_raw[:, columns(i)])
        copy.wait()
        e_high, e_low = halves(held[:, columns(i)])
        parts = mm(e_high, jnp.concatenate([high, low], 0), NT)
        part = parts[:, :64] + parts[:, 64:] + mm(e_low, high, NT)
        if i == 0:
            out[...] = part
        else:
            out[...] += part


def right(p_raw, error):
    return pallas(
        right_body,
        shaped((512, 64)),
        flops=2 * 512 * 4096 * 192,
        bytes_accessed=9 << 20,
        in_specs=[VMEM, HBM],
        out_specs=VMEM,
        scratch_shapes=[pltpu.VMEM((512, 4096), F32), pltpu.SemaphoreType.DMA((8,))],
    )(p_raw, in_hbm(error))


def collect_body(place, term, turned, u0, u1, u2, u3, u_far, out, u_all):
    x, c = place[0], place[1]
    for a, d in RELATIVE:
        u = (u0, u1, u2, u3)[d][...] if a == 0 else u_far[64 * d : 64 * d + 64, :]
        first = pl.multiple_of(chunk_of(x, c, a, d) * 128, 128)
        for n, part in enumerate(thirds(u)):
            u_all[64 * n : 64 * n + 64, pl.ds(first, 128)] = part
    parts = mm(u_all[...], turned[...], NT)
    out[...] = term[...].T + (parts[:64] + parts[64:128] + parts[128:])


def collect(place, term, turned, u_near, u_far):
    return pallas(
        collect_body,
        shaped((64, 512)),
        flops=2 * 192 * 1024 * 512,
        bytes_accessed=2 << 20,
        in_specs=[SMEM] + [VMEM] * 7,
        out_specs=VMEM,
        scratch_shapes=[pltpu.VMEM((192, 1024), BF16)],
    )(place, term, turned, *u_near, u_far)


def solve_body(p_raw, inverse, out):
    squares = jnp.zeros((192, 192), F32)
    for i in range(4):
        stack = jnp.concatenate(thirds(p_raw[:, 1024 * i : 1024 * i + 1024]), 0)
        squares += mm(stack, stack, NT)
    gram = squares[:64, :64] + (
        (squares[:64, 64:128] + squares[64:128, :64]) + (squares[:64, 128:] + squares[128:, :64] + squares[64:128, 64:128])
    )
    same = lax.broadcasted_iota(jnp.int32, (64, 64), 0) == lax.broadcasted_iota(jnp.int32, (64, 64), 1)
    row = lax.broadcasted_iota(jnp.int32, (64, 128), 0)
    both = jnp.concatenate([gram, jnp.where(same, 1.0, 0.0).astype(F32)], 1)
    for k in range(64):
        scale = both[:, k : k + 1] / both[k : k + 1, k : k + 1]
        both = both - jnp.where(row > k, scale * both[k : k + 1, :], 0.0)
    diagonal = jnp.sum(jnp.where(same, both[:, :64], 0.0), 1, keepdims=True)
    solved = both[:, 64:] / jnp.sqrt(diagonal)
    inverse[...] = solved
    for i in range(4):
        at = slice(1024 * i, 1024 * i + 1024)
        high, low = halves(mm(solved, p_raw[:, at], NN, lax.Precision.HIGHEST))
        out[:, at] = jnp.concatenate([high, low, high], 0)


def solve(p_raw):
    return pallas(
        solve_body,
        [shaped((64, 64)), shaped((192, 4096), BF16)],
        flops=8 << 20,
        bytes_accessed=25 << 20,
        in_specs=[VMEM],
        out_specs=[VMEM] * 2,
    )(p_raw)


def last_body(inverse, w, turned, p, error, ctx, q_out, out, held, held_ctx, arrived, arrived_ctx, left_here):
    copies = list(zip(fetch(error, held, arrived), fetch(ctx, held_ctx, arrived_ctx)))
    q = mm(inverse[...], w[...], NN, lax.Precision.HIGHEST) * (1.0 / 16)
    q_out[...] = q
    high, low = halves(q.T)
    q_split = jnp.concatenate([high, high, low], 1)
    stores = []
    for i, (copy, copy_ctx) in enumerate(copies):
        copy_ctx.wait()
        product = mm(turned[...], held_ctx[:, columns(i)])
        approx = mm(q_split, p[:, columns(i)])
        copy.wait()
        held[:, columns(i)] = (held[:, columns(i)] + product) - approx
        stores.append(pltpu.make_async_copy(held.at[:, columns(i)], out.at[:, columns(i)], left_here.at[i]))
        stores[-1].start()
    for store in stores:
        store.wait()


def last(inverse, w, turned, p, error, ctx):
    return pallas(
        last_body,
        [shaped((64, 512)), shaped((512, 4096))],
        flops=2 * 512 * 4096 * 1216,
        bytes_accessed=27 << 20,
        mib=32,
        in_specs=[VMEM] * 4 + [HBM] * 2,
        out_specs=[VMEM, HBM],
        scratch_shapes=[pltpu.VMEM((512, 4096), F32), pltpu.VMEM((1024, 4096), BF16)] + [pltpu.SemaphoreType.DMA((8,))] * 3,
    )(inverse, w, turned, p, in_hbm(error), in_hbm(ctx))


def share_body(place, tokens, *refs):
    slabs, outs, whole = refs[:8], refs[8:12], refs[12]
    x, c, y, z = place[0], place[1], place[2], place[3]
    for e in range(4):
        total = jnp.zeros((512, 256), F32)
        for a in range(2):
            for d in range(4):
                at = pl.ds(pl.multiple_of(chunk_of(x, c, a, 4 - d) * 512, 512), 512)
                total += mm(tokens[:, :, at].reshape(512, 512), slabs[4 * a + e][d], NT)
        whole[:, pl.ds(pl.multiple_of(lax.rem(y + e, 4) * 256, 256), 256)] = total.astype(BF16)
    for d, out in enumerate(outs):
        out[...] = whole[pl.ds(pl.multiple_of(lax.rem(z + d, 4) * 128, 128), 128), :]


def share(place, tokens, mine, theirs):
    return pallas(
        share_body,
        [shaped((128, 1024), BF16)] * 4,
        flops=2 * 512 * 1024 * 4096,
        bytes_accessed=12 << 20,
        mib=24,
        in_specs=[SMEM] + [VMEM] * 9,
        out_specs=[VMEM] * 4,
        scratch_shapes=[pltpu.VMEM((512, 1024), BF16)],
    )(place, tokens, *mine, *theirs)


def pair_sum(values):
    return (values[0] + values[2]) + (values[1] + values[3])


def local(ctx, grad_out, weight, error, q_init):
    j, k = lax.axis_index("fsdp"), lax.axis_index("dp")
    x, c, y, z = j // 2, j % 2, k // 4, k % 4
    place = jnp.stack([x, c, y, z]).astype(jnp.int32)
    error = error[0]

    groups = [[e * 4 + f for f in range(4)] for e in range(4)]
    tokens = lax.all_gather(grad_out, "dp", axis_index_groups=groups)

    qt = q_init.T
    q_near = [qt] + [along_x(qt, -d) for d in (1, 2, 3)]
    piece = lax.dynamic_slice_in_dim(weight, z * 1024 + y * 256, 256, 0)
    pieces = [piece, along_x(piece, 1), along_x(after(piece, q_near[1]), 2), along_x(piece, 3)]
    term = error_left(place, qt, error)
    q_far = other_core(jnp.concatenate([qt, after(q_near[1], term, pieces[1], pieces[3]), *q_near[2:]], 0))
    near, far = left(place, q_near, after(q_far, pieces[2]), grad_out, ctx, term)
    half = near + other_core(far)

    sends = cut(place, grad_out)
    moved = [sends[0]] + [along_x(after(sends[d], near), d) if d != 2 else None for d in (1, 2, 3)]
    blocks = [half[:8]] + [along_z(half[8 * d : 8 * d + 8], d) for d in (1, 2, 3)]
    blocks[3] = after(blocks[3], moved[1], moved[3])
    summed = pair_sum(blocks)
    moved[2] = along_x(after(sends[2], summed), 2)
    w0 = after(jnp.stack(pieces), half)
    over_y = [summed] + [along_y(summed, d) for d in (1, 2, 3)]
    their0 = other_core(after(w0, summed))
    over_y[3] = after(over_y[3], moved[2], their0)
    summed = pair_sum(over_y)
    w1, w3 = [along_y(after(w0, summed), d) for d in (-1, 1)]
    far_columns = other_core(after(jnp.stack([m[1] for m in moved]), summed))
    over_x = [summed] + [along_x(summed, d) for d in (1, 2, 3)]
    ctx_all = lax.all_gather(after(ctx, summed, tokens), "fsdp", axis=0, tiled=True)
    turned = turn(place, moved, far_columns)
    over_x[3] = after(over_x[3], turned)
    rows = pair_sum(over_x)
    p_near = [rows] + [along_z(rows, -d) for d in (1, 2, 3)]
    p_far = other_core(jnp.concatenate(p_near, 0))

    p_raw, u = middle(place, p_near, after(p_far, w1, w3), ctx)
    w2 = along_y(after(w0, w1, w3), 2)
    u_near = [u] + [along_x(u, -d) for d in (1, 2, 3)]
    w_term = right(p_raw, error)
    u_far = other_core(jnp.concatenate([u, u_near[1], u_near[2], after(u_near[3], w_term)], 0))
    their1, their3 = other_core(after(w1, u)), other_core(after(w3, u))
    w = collect(place, after(w_term, their1, their3), turned, u_near, u_far)
    w = [w] + [along_z(w, d) for d in (1, 2, 3)]
    inverse, p = solve(p_raw)
    w = pair_sum([w[0], w[1], w[2], after(w[3], p)])
    their2 = other_core(after(w2, w))
    w = [w] + [along_y(w, d) for d in (1, 2, 3)]
    outs = share(place, tokens, [w0, w1, w2, w3], [their0, their1, their2, their3])
    w = pair_sum([w[0], w[1], w[2], after(w[3], outs[0])])
    outs = [outs[0]] + [along_z(outs[d], d) for d in (1, 2, 3)]
    q_factor, new_error = last(inverse, w, turned, p, error, ctx_all)
    grad_ctx = join(place, [outs[0], outs[3], outs[2], after(outs[1], q_factor)])
    return (grad_ctx, q_factor.T, new_error[None])


def solution(mesh):
    in_specs = (
        P(("dp", "fsdp"), None),
        P(("dp", "fsdp"), None),
        P(None, "fsdp"),
        P("dp", "fsdp", None),
        P("fsdp", None),
    )
    out_specs = (P(("dp", "fsdp"), None), P("fsdp", None), P("dp", "fsdp", None))
    return jax.shard_map(local, mesh=mesh, in_specs=in_specs, out_specs=out_specs, check_vma=False)
```

```python
import functools

import jax
import jax.numpy as jnp
from jax import lax
from jax.experimental import pallas as pl
from jax.experimental.pallas import tpu as pltpu
from jax.sharding import PartitionSpec as P

F32, BF16 = jnp.float32, jnp.bfloat16
VMEM = pl.BlockSpec(memory_space=pltpu.VMEM)
SMEM = pl.BlockSpec(memory_space=pltpu.SMEM)
HBM = pl.BlockSpec(memory_space=pltpu.HBM)
RELATIVE = [(a, d) for a in range(2) for d in range(4)]
NT = (((1,), (1,)), ((), ()))
NN = (((1,), (0,)), ((), ()))


def mm(lhs, rhs, dims=NN, precision=None):
    return lax.dot_general(lhs, rhs, dims, precision=precision, preferred_element_type=F32)


def halves(value):
    high = value.astype(BF16)
    return high, (value - high.astype(F32)).astype(BF16)


def thirds(value):
    high = value.astype(BF16)
    rest = value - high.astype(F32)
    mid = rest.astype(BF16)
    return high, mid, (rest - mid.astype(F32)).astype(BF16)


def along_x(value, d):
    return lax.ppermute(value, "fsdp", [(i, ((i // 2 + d) % 4) * 2 + i % 2) for i in range(8)])


def along_y(value, d):
    return lax.ppermute(value, "dp", [(i, ((i // 4 + d) % 4) * 4 + i % 4) for i in range(16)])


def along_z(value, d):
    return lax.ppermute(value, "dp", [(i, (i // 4) * 4 + (i % 4 + d) % 4) for i in range(16)])


def other_core(value):
    return lax.ppermute(value, "fsdp", [(i, i ^ 1) for i in range(8)])


def to_relative(value, a, d):
    return lax.ppermute(value, "fsdp", [(i, ((i // 2 + d) % 4) * 2 + (i % 2 ^ a)) for i in range(8)])


def pallas(body, out_shape, mib=16, **kw):
    return pl.pallas_call(
        body,
        out_shape=out_shape,
        compiler_params=pltpu.CompilerParams(vmem_limit_bytes=mib * 2**20),
        cost_estimate=pl.CostEstimate(flops=0, bytes_accessed=0, transcendentals=0),
        **kw,
    )


def in_hbm(value):
    return pltpu.with_memory_space_constraint(value, pltpu.HBM)


def shaped(shape, dtype=F32):
    return jax.ShapeDtypeStruct(shape, dtype)


def after(value, *earlier):
    return lax.optimization_barrier((value, *earlier))[0]


def chunk_of(x, c, a, d):
    return lax.rem(x + d, 4) * 2 + (c ^ a)


def rank_row(y, c, a, d):
    return pl.multiple_of((c ^ a) * 32 + lax.rem(y + d, 4) * 8, 8)


def cut_body(place, grad, *outs):
    x, c = place[0], place[1]
    for d, out in enumerate(outs):
        for a in range(2):
            out[a] = grad[:, pl.ds(pl.multiple_of(chunk_of(x, c, a, d) * 512, 512), 512)]


def cut(place, grad):
    return pallas(cut_body, [shaped((2, 128, 512), BF16)] * 4, in_specs=[SMEM, VMEM], out_specs=[VMEM] * 4)(place, grad)


def sort_body(c0, c1, c2, c3, near, far, done):
    copies = []
    for d, chunk in enumerate((c0, c1, c2, c3)):
        for a, out in enumerate((near, far)):
            copies.append(pltpu.make_async_copy(chunk.at[a], out.at[d], done.at[a, d]))
            copies[-1].start()
    for copy in copies:
        copy.wait()


def sort(chunks):
    return pallas(
        sort_body,
        [shaped((4, 128, 512), BF16)] * 2,
        in_specs=[HBM] * 4,
        out_specs=[VMEM] * 2,
        scratch_shapes=[pltpu.SemaphoreType.DMA((2, 4))],
    )(*[in_hbm(chunk) for chunk in chunks])


def columns(i, blocks=4):
    return slice(4096 // blocks * i, 4096 // blocks * (i + 1))


class Fetch:
    def __init__(self, source, held, arrived, ahead, blocks=4):
        parts = [columns(i, blocks) for i in range(blocks)]
        self.copies = [pltpu.make_async_copy(source.at[:, at], held.at[:, at], arrived.at[i]) for i, at in enumerate(parts)]
        self.ahead = ahead
        for copy in self.copies[:ahead]:
            copy.start()

    def wait(self, i):
        if i + self.ahead < len(self.copies):
            self.copies[i + self.ahead].start()
        self.copies[i].wait()


def error_left_body(place, qt, error, out, held, arrived, pieces):
    c, y = place[1], place[2]
    blocks = Fetch(error, held, arrived, 3)
    for n, (a, d) in enumerate(RELATIVE):
        rows = qt[pl.ds(rank_row(y, c, a, d), 8), :]
        high = rows.astype(BF16).astype(F32)
        pieces[8 * n : 8 * n + 8, :] = high
        pieces[64 + 8 * n : 72 + 8 * n, :] = rows - high
    q = pieces[...].astype(BF16)
    for i in range(4):
        blocks.wait(i)
        high, low = halves(held[:, columns(i)])
        first = mm(q, high)
        out[:, columns(i)] = first[:64] + first[64:] + mm(q[:64], low)


def error_left(place, qt, error):
    return pallas(
        error_left_body,
        shaped((64, 4096)),
        in_specs=[SMEM, VMEM, HBM],
        out_specs=VMEM,
        scratch_shapes=[pltpu.VMEM((512, 4096), F32), pltpu.SemaphoreType.DMA((4,)), pltpu.VMEM((128, 512), F32)],
    )(place, qt, in_hbm(error))


def left_body(place, q0, q1, q2, q3, q_far, grad, ctx, term, near, far, g_abs, g_rel):
    x, c, y = place[0], place[1], place[2]
    total = jnp.zeros((64, 128), F32)
    for a, d in RELATIVE:
        q = (q0, q1, q2, q3)[d][...] if a == 0 else q_far[64 * d : 64 * d + 64, :]
        chunk = grad[:, pl.ds(pl.multiple_of(chunk_of(x, c, a, d) * 512, 512), 512)]
        parts = mm(jnp.concatenate(thirds(q), 0), chunk, NT)
        total += parts[:64] + parts[64:128] + parts[128:]
    g_abs[...] = total
    for n, (a, d) in enumerate(RELATIVE):
        g_rel[8 * n : 8 * n + 8, :] = g_abs[pl.ds(rank_row(y, c, a, d), 8), :]
    g = jnp.concatenate(thirds(g_rel[...]), 0)
    for i in range(4):
        at = slice(1024 * i, 1024 * i + 1024)
        parts = mm(g, ctx[:, at])
        whole = term[:, at] + (parts[:64] + parts[64:128] + parts[128:])
        near[:, at] = whole[:32]
        far[:, at] = whole[32:]


def left(place, q_near, q_far, grad, ctx, term):
    return pallas(
        left_body,
        [shaped((32, 4096))] * 2,
        in_specs=[SMEM] + [VMEM] * 8,
        out_specs=[VMEM] * 2,
        scratch_shapes=[pltpu.VMEM((64, 128), F32)] * 2,
    )(place, *q_near, q_far, grad, ctx, term)


def join_body(place, v0, v1, v2, v3, out, done):
    copies = []
    for d, value in enumerate((v0, v1, v2, v3)):
        at = pl.ds(pl.multiple_of(lax.rem(place[3] + d, 4) * 1024, 1024), 1024)
        copies.append(pltpu.make_async_copy(value, out.at[:, at], done.at[d]))
        copies[-1].start()
    for copy in copies:
        copy.wait()


def join(place, values):
    return pallas(
        join_body,
        shaped((128, 4096), BF16),
        in_specs=[SMEM] + [VMEM] * 4,
        out_specs=HBM,
        scratch_shapes=[pltpu.SemaphoreType.DMA((4,))],
    )(place, *values)


def turn_body(place, near, far, out):
    x, c = place[0], place[1]
    for a, d in RELATIVE:
        chunk = far[d] if a else near[d]
        out[:, pl.ds(pl.multiple_of(chunk_of(x, c, a, 4 - d) * 128, 128), 128)] = chunk.T


def turn(place, near, far):
    return pallas(
        turn_body, shaped((512, 1024), BF16), in_specs=[SMEM, VMEM, VMEM], out_specs=VMEM
    )(place, near, far)


def middle_body(place, p0, p1, p2, p3, p_far, ctx, p_out, u_out):
    c, y = place[1], place[2]
    for a, d in RELATIVE:
        p_out[pl.ds(rank_row(y, c, a, d), 8), :] = (p0, p1, p2, p3)[d][...] if a == 0 else p_far[8 * d : 8 * d + 8, :]
    u = jnp.zeros((64, 128), F32)
    for i in range(4):
        at = slice(1024 * i, 1024 * i + 1024)
        parts = mm(jnp.concatenate(thirds(p_out[:, at]), 0), ctx[:, at], NT)
        u += parts[:64] + parts[64:128] + parts[128:]
    u_out[...] = u


def middle(place, p_near, p_far, ctx):
    return pallas(
        middle_body,
        [shaped((64, 4096)), shaped((64, 128))],
        in_specs=[SMEM] + [VMEM] * 6,
        out_specs=[VMEM] * 2,
    )(place, *p_near, p_far, ctx)


def right_body(p_raw, error, out, held, arrived):
    blocks = Fetch(error, held, arrived, 3)
    for i in range(4):
        high, low = halves(p_raw[:, columns(i)])
        blocks.wait(i)
        e_high, e_low = halves(held[:, columns(i)])
        parts = mm(e_high, jnp.concatenate([high, low], 0), NT)
        part = parts[:, :64] + parts[:, 64:] + mm(e_low, high, NT)
        if i == 0:
            out[...] = part
        else:
            out[...] += part


def right(p_raw, error):
    return pallas(
        right_body,
        shaped((512, 64)),
        in_specs=[VMEM, HBM],
        out_specs=VMEM,
        scratch_shapes=[pltpu.VMEM((512, 4096), F32), pltpu.SemaphoreType.DMA((4,))],
    )(p_raw, in_hbm(error))


def collect_body(place, term, turned, u0, u1, u2, u3, u_far, out, u_all):
    x, c = place[0], place[1]
    for a, d in RELATIVE:
        u = (u0, u1, u2, u3)[d][...] if a == 0 else u_far[64 * d : 64 * d + 64, :]
        first = pl.multiple_of(chunk_of(x, c, a, d) * 128, 128)
        for n, part in enumerate(thirds(u)):
            u_all[64 * n : 64 * n + 64, pl.ds(first, 128)] = part
    parts = mm(u_all[...], turned[...], NT)
    out[...] = term[...].T + (parts[:64] + parts[64:128] + parts[128:])


def collect(place, term, turned, u_near, u_far):
    return pallas(
        collect_body,
        shaped((64, 512)),
        in_specs=[SMEM] + [VMEM] * 7,
        out_specs=VMEM,
        scratch_shapes=[pltpu.VMEM((192, 1024), BF16)],
    )(place, term, turned, *u_near, u_far)


def solve_body(p_raw, inverse, out, p, left_here):
    squares = jnp.zeros((192, 192), F32)
    for i in range(4):
        stack = jnp.concatenate(thirds(p_raw[:, 1024 * i : 1024 * i + 1024]), 0)
        squares += mm(stack, stack, NT)
    gram = squares[:64, :64] + (
        (squares[:64, 64:128] + squares[64:128, :64]) + (squares[:64, 128:] + squares[128:, :64] + squares[64:128, 64:128])
    )
    same = lax.broadcasted_iota(jnp.int32, (64, 64), 0) == lax.broadcasted_iota(jnp.int32, (64, 64), 1)
    row = lax.broadcasted_iota(jnp.int32, (64, 128), 0)
    both = jnp.concatenate([gram, jnp.where(same, 1.0, 0.0).astype(F32)], 1)
    for k in range(64):
        scale = both[:, k : k + 1] / both[k : k + 1, k : k + 1]
        both = both - jnp.where(row > k, scale * both[k : k + 1, :], 0.0)
    diagonal = jnp.sum(jnp.where(same, both[:, :64], 0.0), 1, keepdims=True)
    solved = both[:, 64:] / jnp.sqrt(diagonal)
    inverse[...] = solved
    high, low = halves(solved)
    solved_split = jnp.concatenate([high, high, low], 1)
    for i in range(4):
        at = slice(1024 * i, 1024 * i + 1024)
        high, low = halves(p_raw[:, at])
        high, low = halves(mm(solved_split, jnp.concatenate([high, low, high], 0)))
        p[:, at] = jnp.concatenate([high, low, high], 0)
        pltpu.make_async_copy(p.at[:, at], out.at[:, at], left_here.at[i]).start()
    for i in range(4):
        at = slice(1024 * i, 1024 * i + 1024)
        pltpu.make_async_copy(p.at[:, at], out.at[:, at], left_here.at[i]).wait()


def solve(p_raw):
    return pallas(
        solve_body,
        [shaped((64, 64)), pltpu.HBM((192, 4096), BF16)],
        in_specs=[VMEM],
        out_specs=[VMEM, HBM],
        scratch_shapes=[pltpu.VMEM((192, 4096), BF16), pltpu.SemaphoreType.DMA((4,))],
    )(p_raw)


def last_body(inverse, w, turned, p_far, error, ctx, q_out, out, p, held, held_ctx, arrived, arrived_ctx, left_here, p_here):
    ctx_blocks, blocks = Fetch(ctx, held_ctx, arrived_ctx, 2, 8), Fetch(error, held, arrived, 2, 8)
    p_copy = pltpu.make_async_copy(p_far, p, p_here)
    p_copy.start()
    ctx_blocks.wait(0)
    product = mm(turned[...], held_ctx[:, columns(0, 8)])
    q = mm(inverse[...], w[...], NN, lax.Precision.HIGHEST) * (1.0 / 16)
    q_out[...] = q
    high, low = halves(q)
    q_split = jnp.concatenate([high, high, low], 0).T
    p_copy.wait()
    stores = []
    for i in range(8):
        at = columns(i, 8)
        approx = mm(q_split, p[:, at])
        blocks.wait(i)
        held[:, at] = (held[:, at] + product) - approx
        stores.append(pltpu.make_async_copy(held.at[:, at], out.at[:, at], left_here.at[i]))
        stores[-1].start()
        if i < 7:
            ctx_blocks.wait(i + 1)
            product = mm(turned[...], held_ctx[:, columns(i + 1, 8)])
    for store in stores:
        store.wait()


def last(inverse, w, turned, p, error, ctx):
    return pallas(
        last_body,
        [shaped((64, 512)), shaped((512, 4096))],
        mib=24,
        in_specs=[VMEM] * 3 + [HBM] * 3,
        out_specs=[VMEM, HBM],
        scratch_shapes=[pltpu.VMEM((192, 4096), BF16), pltpu.VMEM((512, 4096), F32), pltpu.VMEM((1024, 4096), BF16)]
        + [pltpu.SemaphoreType.DMA((8,))] * 3
        + [pltpu.SemaphoreType.DMA],
    )(inverse, w, turned, in_hbm(p), in_hbm(error), in_hbm(ctx))


def share_body(place, tokens, *refs):
    slabs, outs, whole = refs[:8], refs[8:12], refs[12]
    x, c, y, z = place[0], place[1], place[2], place[3]
    for e in range(4):
        total = jnp.zeros((512, 256), F32)
        for a in range(2):
            for d in range(4):
                at = pl.ds(pl.multiple_of(chunk_of(x, c, a, 4 - d) * 512, 512), 512)
                total += mm(tokens[:, :, at].reshape(512, 512), slabs[4 * a + e][d], NT)
        whole[:, pl.ds(pl.multiple_of(lax.rem(y + e, 4) * 256, 256), 256)] = total.astype(BF16)
    for d, out in enumerate(outs):
        out[...] = whole[pl.ds(pl.multiple_of(lax.rem(z + d, 4) * 128, 128), 128), :]


def share(place, tokens, mine, theirs):
    return pallas(
        share_body,
        [shaped((128, 1024), BF16)] * 4,
        mib=24,
        in_specs=[SMEM] + [VMEM] * 9,
        out_specs=[VMEM] * 4,
        scratch_shapes=[pltpu.VMEM((512, 1024), BF16)],
    )(place, tokens, *mine, *theirs)


def pair_sum(values):
    return (values[0] + values[2]) + (values[1] + values[3])


def local(ctx, grad_out, weight, error, q_init):
    j, k = lax.axis_index("fsdp"), lax.axis_index("dp")
    x, c, y, z = j // 2, j % 2, k // 4, k % 4
    place = jnp.stack([x, c, y, z]).astype(jnp.int32)
    error = error[0]

    groups = [[e * 4 + f for f in range(4)] for e in range(4)]
    tokens = lax.all_gather(grad_out, "dp", axis_index_groups=groups)

    qt = q_init.T
    q_near = [qt] + [along_x(qt, -d) for d in (1, 2, 3)]
    piece = lax.dynamic_slice_in_dim(weight, z * 1024 + y * 256, 256, 0)
    pieces = [piece, along_x(piece, 1), along_x(after(piece, q_near[1]), 2), along_x(piece, 3)]
    term = error_left(place, qt, error)
    q_far = other_core(jnp.concatenate([qt, after(q_near[1], term, pieces[1], pieces[3]), *q_near[2:]], 0))
    sends = cut(place, grad_out)
    near, far = left(place, q_near, q_far, grad_out, ctx, term)
    chunks = [sends[0]] + [along_x(after(sends[d], *q_near), d) if d != 2 else None for d in (1, 2, 3)]
    half = near + other_core(far)

    chunks[2] = along_x(after(sends[2], half), 2)
    blocks = [half[:8]] + [along_y(half[8 * d : 8 * d + 8], d) for d in (1, 2, 3)]
    blocks[3] = after(blocks[3], pieces[2], chunks[1], chunks[3])
    summed = pair_sum(blocks)
    w0 = after(jnp.stack(pieces), summed)
    w1, w3 = [along_y(w0, d) for d in (-1, 1)]
    over_x = [summed] + [along_x(summed, d) for d in (1, 2, 3)]
    over_x[3] = after(over_x[3], chunks[2])
    summed = pair_sum(over_x)
    near_columns, far_columns = sort([*chunks[:3], after(chunks[3], summed)])
    far_columns = other_core(far_columns)
    turned = turn(place, near_columns, far_columns)
    over_z = [summed] + [along_z(summed, d) for d in (1, 2, 3)]
    over_z[3] = after(over_z[3], w1, w3, turned)
    rows = pair_sum(over_z)
    ctx_all = lax.all_gather(after(ctx, rows, tokens), "fsdp", axis=0, tiled=True)
    p_near = [rows] + [along_y(rows, -d) for d in (1, 2, 3)]
    their1, their3 = other_core(after(w1, rows)), other_core(after(w3, rows))
    p_far = other_core(jnp.concatenate([rows, after(p_near[1], their1, their3), *p_near[2:]], 0))
    w2 = along_y(after(w0, *p_near), 2)

    p_raw, u = middle(place, p_near, p_far, ctx)
    u_near = [u] + [along_x(u, -d) for d in (1, 2, 3)]
    w_term = right(p_raw, error)
    their0 = other_core(after(w0, u))
    u_far = other_core(jnp.concatenate([u, u_near[1], u_near[2], after(u_near[3], w_term, their0)], 0))
    w = collect(place, w_term, turned, u_near, u_far)
    w = [w] + [along_z(w, d) for d in (1, 2, 3)]
    inverse, p = solve(p_raw)
    w = pair_sum([w[0], w[1], w[2], after(w[3], p, w2)])
    their2 = other_core(after(w2, w))
    w = [w] + [along_y(w, d) for d in (1, 2, 3)]
    outs = share(place, tokens, [w0, w1, w2, w3], [their0, their1, their2, their3])
    w = pair_sum([w[0], w[1], w[2], after(w[3], outs[0])])
    outs = [outs[0]] + [along_z(outs[d], d) for d in (1, 2, 3)]
    q_factor, new_error = last(inverse, w, turned, p, error, ctx_all)
    grad_ctx = join(place, [outs[0], outs[3], outs[2], after(outs[1], q_factor)])
    return (grad_ctx, q_factor.T, new_error[None])


def solution(mesh):
    in_specs = (
        P(("dp", "fsdp"), None),
        P(("dp", "fsdp"), None),
        P(None, "fsdp"),
        P("dp", "fsdp", None),
        P("fsdp", None),
    )
    out_specs = (P(("dp", "fsdp"), None), P("fsdp", None), P("dp", "fsdp", None))
    return jax.shard_map(local, mesh=mesh, in_specs=in_specs, out_specs=out_specs, check_vma=False)
```

```python
import functools

import jax
import jax.numpy as jnp
from jax import lax
from jax.experimental import pallas as pl
from jax.experimental.pallas import tpu as pltpu
from jax.sharding import PartitionSpec as P

F32, BF16 = jnp.float32, jnp.bfloat16
VMEM = pl.BlockSpec(memory_space=pltpu.VMEM)
SMEM = pl.BlockSpec(memory_space=pltpu.SMEM)
HBM = pl.BlockSpec(memory_space=pltpu.HBM)
RELATIVE = [(a, d) for a in range(2) for d in range(4)]
NT = (((1,), (1,)), ((), ()))
NN = (((1,), (0,)), ((), ()))


def mm(lhs, rhs, dims=NN, precision=None):
    return lax.dot_general(lhs, rhs, dims, precision=precision, preferred_element_type=F32)


def halves(value):
    high = value.astype(BF16)
    return high, (value - high.astype(F32)).astype(BF16)


def thirds(value):
    high = value.astype(BF16)
    rest = value - high.astype(F32)
    mid = rest.astype(BF16)
    return high, mid, (rest - mid.astype(F32)).astype(BF16)


def along_x(value, d):
    return lax.ppermute(value, "fsdp", [(i, ((i // 2 + d) % 4) * 2 + i % 2) for i in range(8)])


def along_y(value, d):
    return lax.ppermute(value, "dp", [(i, ((i // 4 + d) % 4) * 4 + i % 4) for i in range(16)])


def along_z(value, d):
    return lax.ppermute(value, "dp", [(i, (i // 4) * 4 + (i % 4 + d) % 4) for i in range(16)])


def other_core(value):
    return lax.ppermute(value, "fsdp", [(i, i ^ 1) for i in range(8)])


def to_relative(value, a, d):
    return lax.ppermute(value, "fsdp", [(i, ((i // 2 + d) % 4) * 2 + (i % 2 ^ a)) for i in range(8)])


def pallas(body, out_shape, mib=16, **kw):
    return pl.pallas_call(
        body,
        out_shape=out_shape,
        compiler_params=pltpu.CompilerParams(vmem_limit_bytes=mib * 2**20),
        cost_estimate=pl.CostEstimate(flops=0, bytes_accessed=0, transcendentals=0),
        **kw,
    )


def in_hbm(value):
    return pltpu.with_memory_space_constraint(value, pltpu.HBM)


def shaped(shape, dtype=F32):
    return jax.ShapeDtypeStruct(shape, dtype)


def after(value, *earlier):
    return lax.optimization_barrier((value, *earlier))[0]


def chunk_of(x, c, a, d):
    return lax.rem(x + d, 4) * 2 + (c ^ a)


def rank_row(y, c, a, d):
    return pl.multiple_of((c ^ a) * 32 + lax.rem(y + d, 4) * 8, 8)


def cut_far_body(place, grad, out):
    for d in range(4):
        out[d] = grad[:, pl.ds(pl.multiple_of(chunk_of(place[0], place[1], 1, d) * 512, 512), 512)]


def cut_far(place, grad):
    return pallas(cut_far_body, shaped((4, 128, 512), BF16), in_specs=[SMEM, VMEM], out_specs=VMEM)(place, grad)


def cut_body(place, grad, passed, *outs):
    for d, out in enumerate(outs):
        out[0] = grad[:, pl.ds(pl.multiple_of(chunk_of(place[0], place[1], 0, d) * 512, 512), 512)]
        out[1] = passed[d]


def cut(place, grad, passed):
    return pallas(cut_body, [shaped((2, 128, 512), BF16)] * 4, in_specs=[SMEM, VMEM, VMEM], out_specs=[VMEM] * 4)(place, grad, passed)


def columns(i):
    return slice(1024 * i, 1024 * i + 1024)


class Fetch:
    def __init__(self, source, held, arrived, ahead):
        self.copies = [pltpu.make_async_copy(source.at[:, columns(i)], held.at[:, columns(i)], arrived.at[i]) for i in range(4)]
        self.ahead = ahead
        for copy in self.copies[:ahead]:
            copy.start()

    def wait(self, i):
        if i + self.ahead < len(self.copies):
            self.copies[i + self.ahead].start()
        self.copies[i].wait()


def error_left_body(place, qt, error, out, held, arrived, pieces):
    c, y = place[1], place[2]
    blocks = Fetch(error, held, arrived, 3)
    for n, (a, d) in enumerate(RELATIVE):
        rows = qt[pl.ds(rank_row(y, c, a, d), 8), :]
        high = rows.astype(BF16).astype(F32)
        pieces[8 * n : 8 * n + 8, :] = high
        pieces[64 + 8 * n : 72 + 8 * n, :] = rows - high
    q = pieces[...].astype(BF16)
    for i in range(4):
        blocks.wait(i)
        high, low = halves(held[:, columns(i)])
        first = mm(q, high)
        out[:, columns(i)] = first[:64] + first[64:] + mm(q[:64], low)


def error_left(place, qt, error):
    return pallas(
        error_left_body,
        shaped((64, 4096)),
        in_specs=[SMEM, VMEM, HBM],
        out_specs=VMEM,
        scratch_shapes=[pltpu.VMEM((512, 4096), F32), pltpu.SemaphoreType.DMA((4,)), pltpu.VMEM((128, 512), F32)],
    )(place, qt, in_hbm(error))


def left_body(place, q0, q1, q2, q3, q_far, grad, ctx, term, near, far, g_abs, g_rel):
    x, c, y = place[0], place[1], place[2]
    total = jnp.zeros((64, 128), F32)
    for a, d in RELATIVE:
        q = (q0, q1, q2, q3)[d][...] if a == 0 else q_far[64 * d : 64 * d + 64, :]
        chunk = grad[:, pl.ds(pl.multiple_of(chunk_of(x, c, a, d) * 512, 512), 512)]
        parts = mm(jnp.concatenate(thirds(q), 0), chunk, NT)
        total += parts[:64] + parts[64:128] + parts[128:]
    g_abs[...] = total
    for n, (a, d) in enumerate(RELATIVE):
        g_rel[8 * n : 8 * n + 8, :] = g_abs[pl.ds(rank_row(y, c, a, d), 8), :]
    g = jnp.concatenate(thirds(g_rel[...]), 0)
    for i in range(4):
        at = slice(1024 * i, 1024 * i + 1024)
        parts = mm(g, ctx[:, at])
        whole = term[:, at] + (parts[:64] + parts[64:128] + parts[128:])
        near[:, at] = whole[:32]
        far[:, at] = whole[32:]


def left(place, q_near, q_far, grad, ctx, term):
    return pallas(
        left_body,
        [shaped((32, 4096))] * 2,
        in_specs=[SMEM] + [VMEM] * 8,
        out_specs=[VMEM] * 2,
        scratch_shapes=[pltpu.VMEM((64, 128), F32)] * 2,
    )(place, *q_near, q_far, grad, ctx, term)


def join_body(place, v0, v1, v2, v3, out, done):
    copies = []
    for d, value in enumerate((v0, v1, v2, v3)):
        at = pl.ds(pl.multiple_of(lax.rem(place[3] + d, 4) * 1024, 1024), 1024)
        copies.append(pltpu.make_async_copy(value, out.at[:, at], done.at[d]))
        copies[-1].start()
    for copy in copies:
        copy.wait()


def join(place, values):
    return pallas(
        join_body,
        shaped((128, 4096), BF16),
        in_specs=[SMEM] + [VMEM] * 4,
        out_specs=HBM,
        scratch_shapes=[pltpu.SemaphoreType.DMA((4,))],
    )(place, *values)


def turn_body(place, c0, c1, c2, c3, out, held, done):
    x, c = place[0], place[1]
    copies = [pltpu.make_async_copy(chunk, held.at[d], done.at[d]) for d, chunk in enumerate((c0, c1, c2, c3))]
    for copy in copies:
        copy.start()
    for d, copy in enumerate(copies):
        copy.wait()
        for a in range(2):
            first = pl.multiple_of(chunk_of(x, c, a, 4 - d) * 128, 128)
            out[:, pl.ds(first, 128)] = held[d, a].T


def turn(place, chunks):
    return pallas(
        turn_body,
        shaped((512, 1024), BF16),
        in_specs=[SMEM] + [HBM] * 4,
        out_specs=VMEM,
        scratch_shapes=[pltpu.VMEM((4, 2, 128, 512), BF16), pltpu.SemaphoreType.DMA((4,))],
    )(place, *[in_hbm(chunk) for chunk in chunks])


def middle_body(place, p0, p1, p2, p3, p_far, ctx, p_out, u_out):
    c, y = place[1], place[2]
    for a, d in RELATIVE:
        p_out[pl.ds(rank_row(y, c, a, d), 8), :] = (p0, p1, p2, p3)[d][...] if a == 0 else p_far[8 * d : 8 * d + 8, :]
    u = jnp.zeros((64, 128), F32)
    for i in range(4):
        at = slice(1024 * i, 1024 * i + 1024)
        parts = mm(jnp.concatenate(thirds(p_out[:, at]), 0), ctx[:, at], NT)
        u += parts[:64] + parts[64:128] + parts[128:]
    u_out[...] = u


def middle(place, p_near, p_far, ctx):
    return pallas(
        middle_body,
        [shaped((64, 4096)), shaped((64, 128))],
        in_specs=[SMEM] + [VMEM] * 6,
        out_specs=[VMEM] * 2,
    )(place, *p_near, p_far, ctx)


def right_body(p_raw, error, out, held, arrived):
    blocks = Fetch(error, held, arrived, 3)
    for i in range(4):
        high, low = halves(p_raw[:, columns(i)])
        blocks.wait(i)
        e_high, e_low = halves(held[:, columns(i)])
        parts = mm(e_high, jnp.concatenate([high, low], 0), NT)
        part = parts[:, :64] + parts[:, 64:] + mm(e_low, high, NT)
        if i == 0:
            out[...] = part
        else:
            out[...] += part


def right(p_raw, error):
    return pallas(
        right_body,
        shaped((512, 64)),
        in_specs=[VMEM, HBM],
        out_specs=VMEM,
        scratch_shapes=[pltpu.VMEM((512, 4096), F32), pltpu.SemaphoreType.DMA((4,))],
    )(p_raw, in_hbm(error))


def collect_body(place, term, turned, u0, u1, u2, u3, u_far, out, u_all):
    x, c = place[0], place[1]
    for a, d in RELATIVE:
        u = (u0, u1, u2, u3)[d][...] if a == 0 else u_far[64 * d : 64 * d + 64, :]
        first = pl.multiple_of(chunk_of(x, c, a, d) * 128, 128)
        for n, part in enumerate(thirds(u)):
            u_all[64 * n : 64 * n + 64, pl.ds(first, 128)] = part
    parts = mm(u_all[...], turned[...], NT)
    out[...] = term[...].T + (parts[:64] + parts[64:128] + parts[128:])


def collect(place, term, turned, u_near, u_far):
    return pallas(
        collect_body,
        shaped((64, 512)),
        in_specs=[SMEM] + [VMEM] * 7,
        out_specs=VMEM,
        scratch_shapes=[pltpu.VMEM((192, 1024), BF16)],
    )(place, term, turned, *u_near, u_far)


def solve_body(p_raw, inverse, out, p, left_here):
    squares = jnp.zeros((192, 192), F32)
    for i in range(4):
        stack = jnp.concatenate(thirds(p_raw[:, 1024 * i : 1024 * i + 1024]), 0)
        squares += mm(stack, stack, NT)
    gram = squares[:64, :64] + (
        (squares[:64, 64:128] + squares[64:128, :64]) + (squares[:64, 128:] + squares[128:, :64] + squares[64:128, 64:128])
    )
    same = lax.broadcasted_iota(jnp.int32, (64, 64), 0) == lax.broadcasted_iota(jnp.int32, (64, 64), 1)
    row = lax.broadcasted_iota(jnp.int32, (64, 128), 0)
    both = jnp.concatenate([gram, jnp.where(same, 1.0, 0.0).astype(F32)], 1)
    for k in range(64):
        scale = both[:, k : k + 1] / both[k : k + 1, k : k + 1]
        both = both - jnp.where(row > k, scale * both[k : k + 1, :], 0.0)
    diagonal = jnp.sum(jnp.where(same, both[:, :64], 0.0), 1, keepdims=True)
    solved = both[:, 64:] / jnp.sqrt(diagonal)
    inverse[...] = solved
    high, low = halves(solved)
    solved_split = jnp.concatenate([high, high, low], 1)
    for i in range(4):
        at = slice(1024 * i, 1024 * i + 1024)
        high, low = halves(p_raw[:, at])
        high, low = halves(mm(solved_split, jnp.concatenate([high, low, high], 0)))
        p[:, at] = jnp.concatenate([high, low, high], 0)
        pltpu.make_async_copy(p.at[:, at], out.at[:, at], left_here.at[i]).start()
    for i in range(4):
        at = slice(1024 * i, 1024 * i + 1024)
        pltpu.make_async_copy(p.at[:, at], out.at[:, at], left_here.at[i]).wait()


def solve(p_raw):
    return pallas(
        solve_body,
        [shaped((64, 64)), pltpu.HBM((192, 4096), BF16)],
        in_specs=[VMEM],
        out_specs=[VMEM, HBM],
        scratch_shapes=[pltpu.VMEM((192, 4096), BF16), pltpu.SemaphoreType.DMA((4,))],
    )(p_raw)


def last_body(inverse, w, turned, p_far, error, ctx, q_out, out, p, held, held_ctx, arrived, arrived_ctx, left_here, p_here):
    ctx_blocks, blocks = Fetch(ctx, held_ctx, arrived_ctx, 1), Fetch(error, held, arrived, 1)
    p_copy = pltpu.make_async_copy(p_far, p, p_here)
    p_copy.start()
    ctx_blocks.wait(0)
    product = mm(turned[...], held_ctx[:, columns(0)])
    q = mm(inverse[...], w[...], NN, lax.Precision.HIGHEST) * (1.0 / 16)
    q_out[...] = q
    high, low = halves(q)
    q_split = jnp.concatenate([high, high, low], 0).T
    p_copy.wait()
    stores = []
    for i in range(4):
        at = columns(i)
        approx = mm(q_split, p[:, at])
        blocks.wait(i)
        held[:, at] = (held[:, at] + product) - approx
        stores.append(pltpu.make_async_copy(held.at[:, at], out.at[:, at], left_here.at[i]))
        stores[-1].start()
        if i < 3:
            ctx_blocks.wait(i + 1)
            product = mm(turned[...], held_ctx[:, columns(i + 1)])
    for store in stores:
        store.wait()


def last(inverse, w, turned, p, error, ctx):
    return pallas(
        last_body,
        [shaped((64, 512)), shaped((512, 4096))],
        mib=24,
        in_specs=[VMEM] * 3 + [HBM] * 3,
        out_specs=[VMEM, HBM],
        scratch_shapes=[pltpu.VMEM((192, 4096), BF16), pltpu.VMEM((512, 4096), F32), pltpu.VMEM((1024, 4096), BF16)]
        + [pltpu.SemaphoreType.DMA((4,))] * 3
        + [pltpu.SemaphoreType.DMA],
    )(inverse, w, turned, in_hbm(p), in_hbm(error), in_hbm(ctx))


def share_body(place, tokens, *refs):
    slabs, outs, (whole, held, done) = [*refs[:8]], refs[8:12], refs[12:]
    copy = pltpu.make_async_copy(slabs[3], held, done)
    copy.start()
    slabs[3] = held
    x, c, y, z = place[0], place[1], place[2], place[3]
    for e in range(4):
        if e == 3:
            copy.wait()
        total = jnp.zeros((512, 256), F32)
        for a in range(2):
            for d in range(4):
                at = pl.ds(pl.multiple_of(chunk_of(x, c, a, 4 - d) * 512, 512), 512)
                total += mm(tokens[:, :, at].reshape(512, 512), slabs[4 * a + e][d], NT)
        whole[:, pl.ds(pl.multiple_of(lax.rem(y + e, 4) * 256, 256), 256)] = total.astype(BF16)
    for d, out in enumerate(outs):
        out[...] = whole[pl.ds(pl.multiple_of(lax.rem(z + d, 4) * 128, 128), 128), :]


def share(place, tokens, mine, theirs):
    return pallas(
        share_body,
        [shaped((128, 1024), BF16)] * 4,
        mib=24,
        in_specs=[SMEM] + [VMEM] * 4 + [HBM] + [VMEM] * 4,
        out_specs=[VMEM] * 4,
        scratch_shapes=[pltpu.VMEM((512, 1024), BF16), pltpu.VMEM((4, 256, 512), BF16), pltpu.SemaphoreType.DMA],
    )(place, tokens, *mine[:3], in_hbm(mine[3]), *theirs)


def pair_sum(values):
    return (values[0] + values[2]) + (values[1] + values[3])


def local(ctx, grad_out, weight, error, q_init):
    j, k = lax.axis_index("fsdp"), lax.axis_index("dp")
    x, c, y, z = j // 2, j % 2, k // 4, k % 4
    place = jnp.stack([x, c, y, z]).astype(jnp.int32)
    error = error[0]

    groups = [[e * 4 + f for f in range(4)] for e in range(4)]
    tokens = lax.all_gather(grad_out, "dp", axis_index_groups=groups)

    qt = q_init.T
    q_near = [qt] + [along_x(qt, -d) for d in (1, 2, 3)]
    piece = lax.dynamic_slice_in_dim(weight, z * 1024 + y * 256, 256, 0)
    pieces = [piece, along_x(piece, 1), along_x(after(piece, q_near[1]), 2), along_x(piece, 3)]
    term = error_left(place, qt, error)
    q_far = other_core(jnp.concatenate([qt, after(q_near[1], term, pieces[1], pieces[3]), *q_near[2:]], 0))
    near, far = left(place, q_near, q_far, grad_out, ctx, term)
    half = near + other_core(far)

    passed = other_core(after(cut_far(place, grad_out), near))
    blocks = [half[:8]] + [along_y(half[8 * d : 8 * d + 8], d) for d in (1, 2, 3)]
    blocks[3] = after(blocks[3], pieces[2], passed)
    summed = pair_sum(blocks)
    w0 = after(jnp.stack(pieces), summed)
    w1, w3 = [along_y(w0, d) for d in (-1, 1)]
    summed = pair_sum([summed] + [along_x(summed, d) for d in (1, 2, 3)])
    sends = cut(place, grad_out, after(passed, summed))
    chunk1, chunk3 = [along_x(sends[d], d) for d in (1, 3)]
    over_z = [summed] + [along_z(summed, d) for d in (1, 2, 3)]
    their0 = other_core(after(w0, summed))
    over_z[3] = after(over_z[3], w1, w3, chunk1, chunk3, their0)
    rows = pair_sum(over_z)
    ctx_all = lax.all_gather(after(ctx, rows, tokens), "fsdp", axis=0, tiled=True)
    p_near = [rows] + [along_y(rows, -d) for d in (1, 2, 3)]
    chunk2 = along_x(after(sends[2], rows), 2)
    their1, their3 = [other_core(after(v, rows)) for v in (w1, w3)]
    p_far = other_core(jnp.concatenate([rows, after(p_near[1], their1, their3, chunk2), *p_near[2:]], 0))
    w2 = along_y(after(w0, *p_near), 2)

    p_raw, u = middle(place, p_near, p_far, ctx)
    u_near = [u] + [along_x(u, -d) for d in (1, 2, 3)]
    w_term = right(p_raw, error)
    turned = turn(place, [sends[0], chunk1, chunk2, chunk3])
    u_far = other_core(jnp.concatenate([u, u_near[1], u_near[2], after(u_near[3], w_term, turned)], 0))
    w = collect(place, w_term, turned, u_near, u_far)
    w = [w] + [along_z(w, d) for d in (1, 2, 3)]
    inverse, p = solve(p_raw)
    w = pair_sum([w[0], w[1], w[2], after(w[3], p, w2)])
    their2 = other_core(after(w2, w))
    w = [w] + [along_y(w, d) for d in (1, 2, 3)]
    outs = share(place, tokens, [w0, w1, w2, w3], [their0, their1, their2, their3])
    w = pair_sum([w[0], w[1], w[2], after(w[3], outs[0])])
    outs = [outs[0]] + [along_z(outs[d], d) for d in (1, 2, 3)]
    q_factor, new_error = last(inverse, w, turned, p, error, ctx_all)
    grad_ctx = join(place, [outs[0], outs[3], outs[2], after(outs[1], q_factor)])
    return (grad_ctx, q_factor.T, new_error[None])


def solution(mesh):
    in_specs = (
        P(("dp", "fsdp"), None),
        P(("dp", "fsdp"), None),
        P(None, "fsdp"),
        P("dp", "fsdp", None),
        P("fsdp", None),
    )
    out_specs = (P(("dp", "fsdp"), None), P("fsdp", None), P("dp", "fsdp", None))
    return jax.shard_map(local, mesh=mesh, in_specs=in_specs, out_specs=out_specs, check_vma=False)
```

```python
import functools

import jax
import jax.numpy as jnp
from jax import lax
from jax.experimental import pallas as pl
from jax.experimental.pallas import tpu as pltpu
from jax.sharding import PartitionSpec as P

F32, BF16 = jnp.float32, jnp.bfloat16
VMEM = pl.BlockSpec(memory_space=pltpu.VMEM)
SMEM = pl.BlockSpec(memory_space=pltpu.SMEM)
HBM = pl.BlockSpec(memory_space=pltpu.HBM)
RELATIVE = [(a, d) for a in range(2) for d in range(4)]
NT = (((1,), (1,)), ((), ()))
NN = (((1,), (0,)), ((), ()))


def mm(lhs, rhs, dims=NN, precision=None):
    return lax.dot_general(lhs, rhs, dims, precision=precision, preferred_element_type=F32)


def halves(value):
    high = value.astype(BF16)
    return high, (value - high.astype(F32)).astype(BF16)


def thirds(value):
    high = value.astype(BF16)
    rest = value - high.astype(F32)
    mid = rest.astype(BF16)
    return high, mid, (rest - mid.astype(F32)).astype(BF16)


def along_x(value, d):
    return lax.ppermute(value, "fsdp", [(i, ((i // 2 + d) % 4) * 2 + i % 2) for i in range(8)])


def along_y(value, d):
    return lax.ppermute(value, "dp", [(i, ((i // 4 + d) % 4) * 4 + i % 4) for i in range(16)])


def along_z(value, d):
    return lax.ppermute(value, "dp", [(i, (i // 4) * 4 + (i % 4 + d) % 4) for i in range(16)])


def other_core(value):
    return lax.ppermute(value, "fsdp", [(i, i ^ 1) for i in range(8)])


def to_relative(value, a, d):
    return lax.ppermute(value, "fsdp", [(i, ((i // 2 + d) % 4) * 2 + (i % 2 ^ a)) for i in range(8)])


def pallas(body, out_shape, mib=16, **kw):
    return pl.pallas_call(
        body,
        out_shape=out_shape,
        compiler_params=pltpu.CompilerParams(vmem_limit_bytes=mib * 2**20),
        cost_estimate=pl.CostEstimate(flops=0, bytes_accessed=0, transcendentals=0),
        **kw,
    )


def in_hbm(value):
    return pltpu.with_memory_space_constraint(value, pltpu.HBM)


def shaped(shape, dtype=F32):
    return jax.ShapeDtypeStruct(shape, dtype)


def after(value, *earlier):
    return lax.optimization_barrier((value, *earlier))[0]


def chunk_of(x, c, a, d):
    return lax.rem(x + d, 4) * 2 + (c ^ a)


def rank_row(y, c, a, d):
    return pl.multiple_of((c ^ a) * 32 + lax.rem(y + d, 4) * 8, 8)


def cut_far_body(place, grad, out):
    for d in range(4):
        out[d] = grad[:, pl.ds(pl.multiple_of(chunk_of(place[0], place[1], 1, d) * 512, 512), 512)]


def cut_far(place, grad):
    return pallas(cut_far_body, shaped((4, 128, 512), BF16), in_specs=[SMEM, VMEM], out_specs=VMEM)(place, grad)


def cut_body(place, grad, passed, *outs):
    for d, out in enumerate(outs):
        out[0] = grad[:, pl.ds(pl.multiple_of(chunk_of(place[0], place[1], 0, d) * 512, 512), 512)]
        out[1] = passed[d]


def cut(place, grad, passed):
    return pallas(cut_body, [shaped((2, 128, 512), BF16)] * 4, in_specs=[SMEM, VMEM, VMEM], out_specs=[VMEM] * 4)(place, grad, passed)


def columns(i):
    return slice(1024 * i, 1024 * i + 1024)


EVEN = [columns(i) for i in range(4)]
ENDS_SMALL = [slice(0, 512), slice(512, 1536), slice(1536, 2560), slice(2560, 3584), slice(3584, 4096)]


class Fetch:
    def __init__(self, source, held, arrived, ahead, parts=EVEN):
        self.copies = [pltpu.make_async_copy(source.at[:, at], held.at[:, at], arrived.at[i]) for i, at in enumerate(parts)]
        self.ahead = ahead
        for copy in self.copies[:ahead]:
            copy.start()

    def wait(self, i):
        if i + self.ahead < len(self.copies):
            self.copies[i + self.ahead].start()
        self.copies[i].wait()


def error_left_body(place, qt, error, out, held, arrived, pieces):
    c, y = place[1], place[2]
    blocks = Fetch(error, held, arrived, 3)
    for n, (a, d) in enumerate(RELATIVE):
        rows = qt[pl.ds(rank_row(y, c, a, d), 8), :]
        high = rows.astype(BF16).astype(F32)
        pieces[8 * n : 8 * n + 8, :] = high
        pieces[64 + 8 * n : 72 + 8 * n, :] = rows - high
    q = pieces[...].astype(BF16)
    for i in range(4):
        blocks.wait(i)
        high, low = halves(held[:, columns(i)])
        first = mm(q, high)
        out[:, columns(i)] = first[:64] + first[64:] + mm(q[:64], low)


def error_left(place, qt, error):
    return pallas(
        error_left_body,
        shaped((64, 4096)),
        in_specs=[SMEM, VMEM, HBM],
        out_specs=VMEM,
        scratch_shapes=[pltpu.VMEM((512, 4096), F32), pltpu.SemaphoreType.DMA((4,)), pltpu.VMEM((128, 512), F32)],
    )(place, qt, in_hbm(error))


def left_body(place, q0, q1, q2, q3, q_far, grad, ctx, term, near, far, g_abs, g_rel):
    x, c, y = place[0], place[1], place[2]
    total = jnp.zeros((64, 128), F32)
    for a, d in RELATIVE:
        q = (q0, q1, q2, q3)[d][...] if a == 0 else q_far[64 * d : 64 * d + 64, :]
        chunk = grad[:, pl.ds(pl.multiple_of(chunk_of(x, c, a, d) * 512, 512), 512)]
        parts = mm(jnp.concatenate(thirds(q), 0), chunk, NT)
        total += parts[:64] + parts[64:128] + parts[128:]
    g_abs[...] = total
    for n, (a, d) in enumerate(RELATIVE):
        g_rel[8 * n : 8 * n + 8, :] = g_abs[pl.ds(rank_row(y, c, a, d), 8), :]
    g = jnp.concatenate(thirds(g_rel[...]), 0)
    for i in range(4):
        at = slice(1024 * i, 1024 * i + 1024)
        parts = mm(g, ctx[:, at])
        whole = term[:, at] + (parts[:64] + parts[64:128] + parts[128:])
        near[:, at] = whole[:32]
        far[:, at] = whole[32:]


def left(place, q_near, q_far, grad, ctx, term):
    return pallas(
        left_body,
        [shaped((32, 4096))] * 2,
        in_specs=[SMEM] + [VMEM] * 8,
        out_specs=[VMEM] * 2,
        scratch_shapes=[pltpu.VMEM((64, 128), F32)] * 2,
    )(place, *q_near, q_far, grad, ctx, term)


def join_body(place, v0, v1, v2, v3, out, done):
    copies = []
    for d, value in enumerate((v0, v1, v2, v3)):
        at = pl.ds(pl.multiple_of(lax.rem(place[3] + d, 4) * 1024, 1024), 1024)
        copies.append(pltpu.make_async_copy(value, out.at[:, at], done.at[d]))
        copies[-1].start()
    for copy in copies:
        copy.wait()


def join(place, values):
    return pallas(
        join_body,
        shaped((128, 4096), BF16),
        in_specs=[SMEM] + [VMEM] * 4,
        out_specs=HBM,
        scratch_shapes=[pltpu.SemaphoreType.DMA((4,))],
    )(place, *values)


def turn_body(place, c0, c1, c2, c3, out, held, done):
    x, c = place[0], place[1]
    copies = [pltpu.make_async_copy(chunk, held.at[d], done.at[d]) for d, chunk in enumerate((c0, c1, c2, c3))]
    for copy in copies:
        copy.start()
    for d, copy in enumerate(copies):
        copy.wait()
        for a in range(2):
            first = pl.multiple_of(chunk_of(x, c, a, 4 - d) * 128, 128)
            out[:, pl.ds(first, 128)] = held[d, a].T


def turn(place, chunks):
    return pallas(
        turn_body,
        shaped((512, 1024), BF16),
        in_specs=[SMEM] + [HBM] * 4,
        out_specs=VMEM,
        scratch_shapes=[pltpu.VMEM((4, 2, 128, 512), BF16), pltpu.SemaphoreType.DMA((4,))],
    )(place, *[in_hbm(chunk) for chunk in chunks])


def middle_body(place, p0, p1, p2, p3, p_far, ctx, p_out, u_out):
    c, y = place[1], place[2]
    for a, d in RELATIVE:
        p_out[pl.ds(rank_row(y, c, a, d), 8), :] = (p0, p1, p2, p3)[d][...] if a == 0 else p_far[8 * d : 8 * d + 8, :]
    u = jnp.zeros((64, 128), F32)
    for i in range(4):
        at = slice(1024 * i, 1024 * i + 1024)
        parts = mm(jnp.concatenate(thirds(p_out[:, at]), 0), ctx[:, at], NT)
        u += parts[:64] + parts[64:128] + parts[128:]
    u_out[...] = u


def middle(place, p_near, p_far, ctx):
    return pallas(
        middle_body,
        [shaped((64, 4096)), shaped((64, 128))],
        in_specs=[SMEM] + [VMEM] * 6,
        out_specs=[VMEM] * 2,
    )(place, *p_near, p_far, ctx)


def right_body(p_raw, error, out, held, arrived):
    blocks = Fetch(error, held, arrived, 3)
    for i in range(4):
        high, low = halves(p_raw[:, columns(i)])
        blocks.wait(i)
        e_high, e_low = halves(held[:, columns(i)])
        parts = mm(e_high, jnp.concatenate([high, low], 0), NT)
        part = parts[:, :64] + parts[:, 64:] + mm(e_low, high, NT)
        if i == 0:
            out[...] = part
        else:
            out[...] += part


def right(p_raw, error):
    return pallas(
        right_body,
        shaped((512, 64)),
        in_specs=[VMEM, HBM],
        out_specs=VMEM,
        scratch_shapes=[pltpu.VMEM((512, 4096), F32), pltpu.SemaphoreType.DMA((4,))],
    )(p_raw, in_hbm(error))


def collect_body(place, term, turned, u0, u1, u2, u3, u_far, out, u_all):
    x, c = place[0], place[1]
    for a, d in RELATIVE:
        u = (u0, u1, u2, u3)[d][...] if a == 0 else u_far[64 * d : 64 * d + 64, :]
        first = pl.multiple_of(chunk_of(x, c, a, d) * 128, 128)
        for n, part in enumerate(thirds(u)):
            u_all[64 * n : 64 * n + 64, pl.ds(first, 128)] = part
    parts = mm(u_all[...], turned[...], NT)
    out[...] = term[...].T + (parts[:64] + parts[64:128] + parts[128:])


def collect(place, term, turned, u_near, u_far):
    return pallas(
        collect_body,
        shaped((64, 512)),
        in_specs=[SMEM] + [VMEM] * 7,
        out_specs=VMEM,
        scratch_shapes=[pltpu.VMEM((192, 1024), BF16)],
    )(place, term, turned, *u_near, u_far)


def solve_body(p_raw, inverse, out, p, left_here):
    squares = jnp.zeros((192, 192), F32)
    for i in range(4):
        stack = jnp.concatenate(thirds(p_raw[:, 1024 * i : 1024 * i + 1024]), 0)
        squares += mm(stack, stack, NT)
    gram = squares[:64, :64] + (
        (squares[:64, 64:128] + squares[64:128, :64]) + (squares[:64, 128:] + squares[128:, :64] + squares[64:128, 64:128])
    )
    same = lax.broadcasted_iota(jnp.int32, (64, 64), 0) == lax.broadcasted_iota(jnp.int32, (64, 64), 1)
    row = lax.broadcasted_iota(jnp.int32, (64, 128), 0)
    both = jnp.concatenate([gram, jnp.where(same, 1.0, 0.0).astype(F32)], 1)
    for k in range(64):
        scale = both[:, k : k + 1] / both[k : k + 1, k : k + 1]
        both = both - jnp.where(row > k, scale * both[k : k + 1, :], 0.0)
    diagonal = jnp.sum(jnp.where(same, both[:, :64], 0.0), 1, keepdims=True)
    solved = both[:, 64:] / jnp.sqrt(diagonal)
    inverse[...] = solved
    high, low = halves(solved)
    solved_split = jnp.concatenate([high, high, low], 1)
    for i in range(4):
        at = slice(1024 * i, 1024 * i + 1024)
        high, low = halves(p_raw[:, at])
        high, low = halves(mm(solved_split, jnp.concatenate([high, low, high], 0)))
        p[:, at] = jnp.concatenate([high, low, high], 0)
        pltpu.make_async_copy(p.at[:, at], out.at[:, at], left_here.at[i]).start()
    for i in range(4):
        at = slice(1024 * i, 1024 * i + 1024)
        pltpu.make_async_copy(p.at[:, at], out.at[:, at], left_here.at[i]).wait()


def solve(p_raw):
    return pallas(
        solve_body,
        [shaped((64, 64)), pltpu.HBM((192, 4096), BF16)],
        in_specs=[VMEM],
        out_specs=[VMEM, HBM],
        scratch_shapes=[pltpu.VMEM((192, 4096), BF16), pltpu.SemaphoreType.DMA((4,))],
    )(p_raw)


def last_body(inverse, w, turned, p_far, error, ctx, q_out, out, p, held, held_ctx, arrived, arrived_ctx, left_here, p_here):
    ctx_blocks, blocks = Fetch(ctx, held_ctx, arrived_ctx, 1, ENDS_SMALL), Fetch(error, held, arrived, 1, ENDS_SMALL)
    p_copy = pltpu.make_async_copy(p_far, p, p_here)
    p_copy.start()
    ctx_blocks.wait(0)
    product = mm(turned[...], held_ctx[:, ENDS_SMALL[0]])
    q = mm(inverse[...], w[...], NN, lax.Precision.HIGHEST) * (1.0 / 16)
    q_out[...] = q
    high, low = halves(q)
    q_split = jnp.concatenate([high, high, low], 0).T
    p_copy.wait()
    stores = []
    for i, at in enumerate(ENDS_SMALL):
        approx = mm(q_split, p[:, at])
        blocks.wait(i)
        held[:, at] = (held[:, at] + product) - approx
        stores.append(pltpu.make_async_copy(held.at[:, at], out.at[:, at], left_here.at[i]))
        stores[-1].start()
        if i < 4:
            ctx_blocks.wait(i + 1)
            product = mm(turned[...], held_ctx[:, ENDS_SMALL[i + 1]])
    for store in stores:
        store.wait()


def last(inverse, w, turned, p, error, ctx):
    return pallas(
        last_body,
        [shaped((64, 512)), shaped((512, 4096))],
        mib=24,
        in_specs=[VMEM] * 3 + [HBM] * 3,
        out_specs=[VMEM, HBM],
        scratch_shapes=[pltpu.VMEM((192, 4096), BF16), pltpu.VMEM((512, 4096), F32), pltpu.VMEM((1024, 4096), BF16)]
        + [pltpu.SemaphoreType.DMA((5,))] * 3
        + [pltpu.SemaphoreType.DMA],
    )(inverse, w, turned, in_hbm(p), in_hbm(error), in_hbm(ctx))


def share_body(place, tokens, *refs):
    slabs, outs, whole = refs[:8], refs[8:12], refs[12]
    x, c, y, z = place[0], place[1], place[2], place[3]
    for e in range(4):
        total = jnp.zeros((512, 256), F32)
        for a in range(2):
            for d in range(4):
                at = pl.ds(pl.multiple_of(chunk_of(x, c, a, 4 - d) * 512, 512), 512)
                total += mm(tokens[:, :, at].reshape(512, 512), slabs[4 * a + e][d], NT)
        whole[:, pl.ds(pl.multiple_of(lax.rem(y + e, 4) * 256, 256), 256)] = total.astype(BF16)
    for d, out in enumerate(outs):
        out[...] = whole[pl.ds(pl.multiple_of(lax.rem(z + d, 4) * 128, 128), 128), :]


def share(place, tokens, mine, theirs):
    return pallas(
        share_body,
        [shaped((128, 1024), BF16)] * 4,
        mib=24,
        in_specs=[SMEM] + [VMEM] * 9,
        out_specs=[VMEM] * 4,
        scratch_shapes=[pltpu.VMEM((512, 1024), BF16)],
    )(place, tokens, *mine, *theirs)


def pair_sum(values):
    return (values[0] + values[2]) + (values[1] + values[3])


def local(ctx, grad_out, weight, error, q_init):
    j, k = lax.axis_index("fsdp"), lax.axis_index("dp")
    x, c, y, z = j // 2, j % 2, k // 4, k % 4
    place = jnp.stack([x, c, y, z]).astype(jnp.int32)
    error = error[0]

    groups = [[e * 4 + f for f in range(4)] for e in range(4)]
    tokens = lax.all_gather(grad_out, "dp", axis_index_groups=groups)

    qt = q_init.T
    q_near = [qt] + [along_x(qt, -d) for d in (1, 2, 3)]
    piece = lax.dynamic_slice_in_dim(weight, z * 1024 + y * 256, 256, 0)
    pieces = [piece, along_x(piece, 1), along_x(after(piece, q_near[1]), 2), along_x(piece, 3)]
    term = error_left(place, qt, error)
    q_far = other_core(jnp.concatenate([qt, after(q_near[1], term, pieces[1], pieces[3]), *q_near[2:]], 0))
    near, far = left(place, q_near, q_far, grad_out, ctx, term)
    half = near + other_core(far)

    passed = other_core(after(cut_far(place, grad_out), near))
    blocks = [half[:8]] + [along_y(half[8 * d : 8 * d + 8], d) for d in (1, 2, 3)]
    blocks[3] = after(blocks[3], pieces[2], passed)
    summed = pair_sum(blocks)
    w0 = after(jnp.stack(pieces), summed)
    w1, w3 = [along_y(w0, d) for d in (-1, 1)]
    summed = pair_sum([summed] + [along_x(summed, d) for d in (1, 2, 3)])
    sends = cut(place, grad_out, after(passed, summed))
    chunk1, chunk3 = [along_x(sends[d], d) for d in (1, 3)]
    over_z = [summed] + [along_z(summed, d) for d in (1, 2, 3)]
    over_z[3] = after(over_z[3], w1, w3, chunk1, chunk3)
    rows = pair_sum(over_z)
    ctx_all = lax.all_gather(after(ctx, rows, tokens), "fsdp", axis=0, tiled=True)
    p_near = [rows] + [along_y(rows, -d) for d in (1, 2, 3)]
    chunk2 = along_x(after(sends[2], rows), 2)
    their1 = other_core(after(w1, rows))
    p_far = other_core(jnp.concatenate([rows, after(p_near[1], their1, chunk2), *p_near[2:]], 0))
    w2 = along_y(after(w0, *p_near), 2)

    turned = turn(place, [sends[0], chunk1, chunk2, chunk3])
    p_raw, u = middle(place, p_near, after(p_far, turned), ctx)
    u_near = [u] + [along_x(u, -d) for d in (1, 2, 3)]
    w_term = right(p_raw, error)
    their0, their3 = other_core(after(w0, u)), other_core(after(w3, u))
    u_far = other_core(jnp.concatenate([u, u_near[1], u_near[2], after(u_near[3], w_term, their0, their3)], 0))
    w = collect(place, w_term, turned, u_near, u_far)
    w = [w] + [along_z(w, d) for d in (1, 2, 3)]
    inverse, p = solve(p_raw)
    w = pair_sum([w[0], w[1], w[2], after(w[3], p, w2)])
    their2 = other_core(after(w2, w))
    w = [w] + [along_y(w, d) for d in (1, 2, 3)]
    outs = share(place, tokens, [w0, w1, w2, w3], [their0, their1, their2, their3])
    w = pair_sum([w[0], w[1], w[2], after(w[3], outs[0])])
    outs = [outs[0]] + [along_z(outs[d], d) for d in (1, 2, 3)]
    q_factor, new_error = last(inverse, w, turned, p, error, ctx_all)
    grad_ctx = join(place, [outs[0], outs[3], outs[2], after(outs[1], q_factor)])
    return (grad_ctx, q_factor.T, new_error[None])


def solution(mesh):
    in_specs = (
        P(("dp", "fsdp"), None),
        P(("dp", "fsdp"), None),
        P(None, "fsdp"),
        P("dp", "fsdp", None),
        P("fsdp", None),
    )
    out_specs = (P(("dp", "fsdp"), None), P("fsdp", None), P("dp", "fsdp", None))
    return jax.shard_map(local, mesh=mesh, in_specs=in_specs, out_specs=out_specs, check_vma=False)
```

```python
import functools

import jax
import jax.numpy as jnp
from jax import lax
from jax.experimental import pallas as pl
from jax.experimental.pallas import tpu as pltpu
from jax.sharding import PartitionSpec as P

F32, BF16 = jnp.float32, jnp.bfloat16
VMEM = pl.BlockSpec(memory_space=pltpu.VMEM)
SMEM = pl.BlockSpec(memory_space=pltpu.SMEM)
HBM = pl.BlockSpec(memory_space=pltpu.HBM)
RELATIVE = [(a, d) for a in range(2) for d in range(4)]
NT = (((1,), (1,)), ((), ()))
NN = (((1,), (0,)), ((), ()))


def mm(lhs, rhs, dims=NN, precision=None):
    return lax.dot_general(lhs, rhs, dims, precision=precision, preferred_element_type=F32)


def halves(value):
    high = value.astype(BF16)
    return high, (value - high.astype(F32)).astype(BF16)


def thirds(value):
    high = value.astype(BF16)
    rest = value - high.astype(F32)
    mid = rest.astype(BF16)
    return high, mid, (rest - mid.astype(F32)).astype(BF16)


def along_x(value, d):
    return lax.ppermute(value, "fsdp", [(i, ((i // 2 + d) % 4) * 2 + i % 2) for i in range(8)])


def along_y(value, d):
    return lax.ppermute(value, "dp", [(i, ((i // 4 + d) % 4) * 4 + i % 4) for i in range(16)])


def along_z(value, d):
    return lax.ppermute(value, "dp", [(i, (i // 4) * 4 + (i % 4 + d) % 4) for i in range(16)])


def other_core(value):
    return lax.ppermute(value, "fsdp", [(i, i ^ 1) for i in range(8)])


def to_relative(value, a, d):
    return lax.ppermute(value, "fsdp", [(i, ((i // 2 + d) % 4) * 2 + (i % 2 ^ a)) for i in range(8)])


def pallas(body, out_shape, mib=16, **kw):
    return pl.pallas_call(
        body,
        out_shape=out_shape,
        compiler_params=pltpu.CompilerParams(vmem_limit_bytes=mib * 2**20),
        cost_estimate=pl.CostEstimate(flops=0, bytes_accessed=0, transcendentals=0),
        **kw,
    )


def in_hbm(value):
    return pltpu.with_memory_space_constraint(value, pltpu.HBM)


def shaped(shape, dtype=F32):
    return jax.ShapeDtypeStruct(shape, dtype)


def after(value, *earlier):
    return lax.optimization_barrier((value, *earlier))[0]


def chunk_of(x, c, a, d):
    return lax.rem(x + d, 4) * 2 + (c ^ a)


def rank_row(y, c, a, d):
    return pl.multiple_of((c ^ a) * 32 + lax.rem(y + d, 4) * 8, 8)


def cut_far_body(place, grad, out):
    for d in range(4):
        out[d] = grad[:, pl.ds(pl.multiple_of(chunk_of(place[0], place[1], 1, d) * 512, 512), 512)]


def cut_far(place, grad):
    return pallas(cut_far_body, shaped((4, 128, 512), BF16), in_specs=[SMEM, VMEM], out_specs=VMEM)(place, grad)


def cut_body(place, grad, passed, *outs):
    for d, out in enumerate(outs):
        out[0] = grad[:, pl.ds(pl.multiple_of(chunk_of(place[0], place[1], 0, d) * 512, 512), 512)]
        out[1] = passed[d]


def cut(place, grad, passed):
    return pallas(cut_body, [shaped((2, 128, 512), BF16)] * 4, in_specs=[SMEM, VMEM, VMEM], out_specs=[VMEM] * 4)(place, grad, passed)


def columns(i):
    return slice(1024 * i, 1024 * i + 1024)


EVEN = [columns(i) for i in range(4)]
ENDS_SMALL = [slice(0, 512), slice(512, 1536), slice(1536, 2560), slice(2560, 3584), slice(3584, 4096)]


class Fetch:
    def __init__(self, source, held, arrived, ahead, parts=EVEN):
        self.copies = [pltpu.make_async_copy(source.at[:, at], held.at[:, at], arrived.at[i]) for i, at in enumerate(parts)]
        self.ahead = ahead
        for copy in self.copies[:ahead]:
            copy.start()

    def wait(self, i):
        if i + self.ahead < len(self.copies):
            self.copies[i + self.ahead].start()
        self.copies[i].wait()


def error_left_body(place, qt, error, out, held, arrived, pieces):
    c, y = place[1], place[2]
    blocks = Fetch(error, held, arrived, 3)
    for n, (a, d) in enumerate(RELATIVE):
        rows = qt[pl.ds(rank_row(y, c, a, d), 8), :]
        high = rows.astype(BF16).astype(F32)
        pieces[8 * n : 8 * n + 8, :] = high
        pieces[64 + 8 * n : 72 + 8 * n, :] = rows - high
    q = pieces[...].astype(BF16)
    for i in range(4):
        blocks.wait(i)
        high, low = halves(held[:, columns(i)])
        first = mm(q, high)
        out[:, columns(i)] = first[:64] + first[64:] + mm(q[:64], low)


def error_left(place, qt, error):
    return pallas(
        error_left_body,
        shaped((64, 4096)),
        in_specs=[SMEM, VMEM, HBM],
        out_specs=VMEM,
        scratch_shapes=[pltpu.VMEM((512, 4096), F32), pltpu.SemaphoreType.DMA((4,)), pltpu.VMEM((128, 512), F32)],
    )(place, qt, in_hbm(error))


def left_body(place, q0, q1, q2, q3, q_far, grad, ctx, term, near, far, g_abs, g_rel):
    x, c, y = place[0], place[1], place[2]
    total = jnp.zeros((64, 128), F32)
    for a, d in RELATIVE:
        q = (q0, q1, q2, q3)[d][...] if a == 0 else q_far[64 * d : 64 * d + 64, :]
        chunk = grad[:, pl.ds(pl.multiple_of(chunk_of(x, c, a, d) * 512, 512), 512)]
        parts = mm(jnp.concatenate(thirds(q), 0), chunk, NT)
        total += parts[:64] + parts[64:128] + parts[128:]
    g_abs[...] = total
    for n, (a, d) in enumerate(RELATIVE):
        g_rel[8 * n : 8 * n + 8, :] = g_abs[pl.ds(rank_row(y, c, a, d), 8), :]
    g = jnp.concatenate(thirds(g_rel[...]), 0)
    for i in range(4):
        at = slice(1024 * i, 1024 * i + 1024)
        parts = mm(g, ctx[:, at])
        whole = term[:, at] + (parts[:64] + parts[64:128] + parts[128:])
        near[:, at] = whole[:32]
        far[:, at] = whole[32:]


def left(place, q_near, q_far, grad, ctx, term):
    return pallas(
        left_body,
        [shaped((32, 4096))] * 2,
        in_specs=[SMEM] + [VMEM] * 8,
        out_specs=[VMEM] * 2,
        scratch_shapes=[pltpu.VMEM((64, 128), F32)] * 2,
    )(place, *q_near, q_far, grad, ctx, term)


def join_body(place, v0, v1, v2, v3, out, done):
    copies = []
    for d, value in enumerate((v0, v1, v2, v3)):
        at = pl.ds(pl.multiple_of(lax.rem(place[3] + d, 4) * 1024, 1024), 1024)
        copies.append(pltpu.make_async_copy(value, out.at[:, at], done.at[d]))
        copies[-1].start()
    for copy in copies:
        copy.wait()


def join(place, values):
    return pallas(
        join_body,
        shaped((128, 4096), BF16),
        in_specs=[SMEM] + [VMEM] * 4,
        out_specs=HBM,
        scratch_shapes=[pltpu.SemaphoreType.DMA((4,))],
    )(place, *values)


def turn_body(place, c0, c1, c2, c3, out, held, done):
    x, c = place[0], place[1]
    copies = [pltpu.make_async_copy(chunk, held.at[d], done.at[d]) for d, chunk in enumerate((c0, c1, c2, c3))]
    for copy in copies:
        copy.start()
    for d, copy in enumerate(copies):
        copy.wait()
        for a in range(2):
            first = pl.multiple_of(chunk_of(x, c, a, 4 - d) * 128, 128)
            out[:, pl.ds(first, 128)] = held[d, a].T


def turn(place, chunks):
    return pallas(
        turn_body,
        shaped((512, 1024), BF16),
        in_specs=[SMEM] + [HBM] * 4,
        out_specs=VMEM,
        scratch_shapes=[pltpu.VMEM((4, 2, 128, 512), BF16), pltpu.SemaphoreType.DMA((4,))],
    )(place, *[in_hbm(chunk) for chunk in chunks])


def middle_body(place, p0, p1, p2, p3, p_far, ctx, p_out, u_out):
    c, y = place[1], place[2]
    for a, d in RELATIVE:
        p_out[pl.ds(rank_row(y, c, a, d), 8), :] = (p0, p1, p2, p3)[d][...] if a == 0 else p_far[8 * d : 8 * d + 8, :]
    u = jnp.zeros((64, 128), F32)
    for i in range(4):
        at = slice(1024 * i, 1024 * i + 1024)
        parts = mm(jnp.concatenate(thirds(p_out[:, at]), 0), ctx[:, at], NT)
        u += parts[:64] + parts[64:128] + parts[128:]
    u_out[...] = u


def middle(place, p_near, p_far, ctx):
    return pallas(
        middle_body,
        [shaped((64, 4096)), shaped((64, 128))],
        in_specs=[SMEM] + [VMEM] * 6,
        out_specs=[VMEM] * 2,
    )(place, *p_near, p_far, ctx)


def right_body(p_raw, error, out, held, arrived):
    blocks = Fetch(error, held, arrived, 2, ENDS_SMALL)
    for i, at in enumerate(ENDS_SMALL):
        high, low = halves(p_raw[:, at])
        blocks.wait(i)
        e_high, e_low = halves(held[:, at])
        parts = mm(e_high, jnp.concatenate([high, low], 0), NT)
        part = parts[:, :64] + parts[:, 64:] + mm(e_low, high, NT)
        if i == 0:
            out[...] = part
        else:
            out[...] += part


def right(p_raw, error):
    return pallas(
        right_body,
        shaped((512, 64)),
        in_specs=[VMEM, HBM],
        out_specs=VMEM,
        scratch_shapes=[pltpu.VMEM((512, 4096), F32), pltpu.SemaphoreType.DMA((5,))],
    )(p_raw, in_hbm(error))


def collect_body(place, term, turned, u0, u1, u2, u3, u_far, out, u_all):
    x, c = place[0], place[1]
    for a, d in RELATIVE:
        u = (u0, u1, u2, u3)[d][...] if a == 0 else u_far[64 * d : 64 * d + 64, :]
        first = pl.multiple_of(chunk_of(x, c, a, d) * 128, 128)
        for n, part in enumerate(thirds(u)):
            u_all[64 * n : 64 * n + 64, pl.ds(first, 128)] = part
    parts = mm(u_all[...], turned[...], NT)
    out[...] = term[...].T + (parts[:64] + parts[64:128] + parts[128:])


def collect(place, term, turned, u_near, u_far):
    return pallas(
        collect_body,
        shaped((64, 512)),
        in_specs=[SMEM] + [VMEM] * 7,
        out_specs=VMEM,
        scratch_shapes=[pltpu.VMEM((192, 1024), BF16)],
    )(place, term, turned, *u_near, u_far)


def solve_body(p_raw, inverse, out, p, left_here):
    squares = jnp.zeros((192, 192), F32)
    for i in range(4):
        stack = jnp.concatenate(thirds(p_raw[:, 1024 * i : 1024 * i + 1024]), 0)
        squares += mm(stack, stack, NT)
    gram = squares[:64, :64] + (
        (squares[:64, 64:128] + squares[64:128, :64]) + (squares[:64, 128:] + squares[128:, :64] + squares[64:128, 64:128])
    )
    same = lax.broadcasted_iota(jnp.int32, (64, 64), 0) == lax.broadcasted_iota(jnp.int32, (64, 64), 1)
    row = lax.broadcasted_iota(jnp.int32, (64, 128), 0)
    both = jnp.concatenate([gram, jnp.where(same, 1.0, 0.0).astype(F32)], 1)
    for k in range(0, 64, 2):
        first, second = both[k : k + 1, :], both[k + 1 : k + 2, :]
        column, next_column = both[:, k : k + 1], both[:, k + 1 : k + 2]
        scale = 1.0 / first[:, k : k + 1]
        ratio = second[:, k : k + 1] * scale
        second = second - ratio * first
        next_column = next_column - ratio * column
        next_scale = 1.0 / second[:, k + 1 : k + 2]
        both = both - (
            jnp.where(row > k, (column * scale) * first, 0.0) + jnp.where(row > k + 1, (next_column * next_scale) * second, 0.0)
        )
    diagonal = jnp.sum(jnp.where(same, both[:, :64], 0.0), 1, keepdims=True)
    solved = both[:, 64:] / jnp.sqrt(diagonal)
    inverse[...] = solved
    high, low = halves(solved)
    solved_split = jnp.concatenate([high, high, low], 1)
    for i in range(4):
        at = slice(1024 * i, 1024 * i + 1024)
        high, low = halves(p_raw[:, at])
        high, low = halves(mm(solved_split, jnp.concatenate([high, low, high], 0)))
        p[:, at] = jnp.concatenate([high, low, high], 0)
        pltpu.make_async_copy(p.at[:, at], out.at[:, at], left_here.at[i]).start()
    for i in range(4):
        at = slice(1024 * i, 1024 * i + 1024)
        pltpu.make_async_copy(p.at[:, at], out.at[:, at], left_here.at[i]).wait()


def solve(p_raw):
    return pallas(
        solve_body,
        [shaped((64, 64)), pltpu.HBM((192, 4096), BF16)],
        in_specs=[VMEM],
        out_specs=[VMEM, HBM],
        scratch_shapes=[pltpu.VMEM((192, 4096), BF16), pltpu.SemaphoreType.DMA((4,))],
    )(p_raw)


def last_body(inverse, w, turned, p_far, error, ctx, q_out, out, p, held, held_ctx, arrived, arrived_ctx, left_here, p_here):
    ctx_blocks, blocks = Fetch(ctx, held_ctx, arrived_ctx, 1, ENDS_SMALL), Fetch(error, held, arrived, 1, ENDS_SMALL)
    p_copy = pltpu.make_async_copy(p_far, p, p_here)
    p_copy.start()
    ctx_blocks.wait(0)
    product = mm(turned[...], held_ctx[:, ENDS_SMALL[0]])
    q = mm(inverse[...], w[...], NN, lax.Precision.HIGHEST) * (1.0 / 16)
    q_out[...] = q
    high, low = halves(q)
    q_split = jnp.concatenate([high, high, low], 0).T
    p_copy.wait()
    stores = []
    for i, at in enumerate(ENDS_SMALL):
        approx = mm(q_split, p[:, at])
        blocks.wait(i)
        held[:, at] = (held[:, at] + product) - approx
        stores.append(pltpu.make_async_copy(held.at[:, at], out.at[:, at], left_here.at[i]))
        stores[-1].start()
        if i < 4:
            ctx_blocks.wait(i + 1)
            product = mm(turned[...], held_ctx[:, ENDS_SMALL[i + 1]])
    for store in stores:
        store.wait()


def last(inverse, w, turned, p, error, ctx):
    return pallas(
        last_body,
        [shaped((64, 512)), shaped((512, 4096))],
        mib=24,
        in_specs=[VMEM] * 3 + [HBM] * 3,
        out_specs=[VMEM, HBM],
        scratch_shapes=[pltpu.VMEM((192, 4096), BF16), pltpu.VMEM((512, 4096), F32), pltpu.VMEM((1024, 4096), BF16)]
        + [pltpu.SemaphoreType.DMA((5,))] * 3
        + [pltpu.SemaphoreType.DMA],
    )(inverse, w, turned, in_hbm(p), in_hbm(error), in_hbm(ctx))


def share_body(place, tokens, *refs):
    slabs, outs, whole = refs[:8], refs[8:12], refs[12]
    x, c, y, z = place[0], place[1], place[2], place[3]
    for e in range(4):
        total = jnp.zeros((512, 256), F32)
        for a in range(2):
            for d in range(4):
                at = pl.ds(pl.multiple_of(chunk_of(x, c, a, 4 - d) * 512, 512), 512)
                total += mm(tokens[:, :, at].reshape(512, 512), slabs[4 * a + e][d], NT)
        whole[:, pl.ds(pl.multiple_of(lax.rem(y + e, 4) * 256, 256), 256)] = total.astype(BF16)
    for d, out in enumerate(outs):
        out[...] = whole[pl.ds(pl.multiple_of(lax.rem(z + d, 4) * 128, 128), 128), :]


def share(place, tokens, mine, theirs):
    return pallas(
        share_body,
        [shaped((128, 1024), BF16)] * 4,
        mib=24,
        in_specs=[SMEM] + [VMEM] * 9,
        out_specs=[VMEM] * 4,
        scratch_shapes=[pltpu.VMEM((512, 1024), BF16)],
    )(place, tokens, *mine, *theirs)


def pair_sum(values):
    return (values[0] + values[2]) + (values[1] + values[3])


def local(ctx, grad_out, weight, error, q_init):
    j, k = lax.axis_index("fsdp"), lax.axis_index("dp")
    x, c, y, z = j // 2, j % 2, k // 4, k % 4
    place = jnp.stack([x, c, y, z]).astype(jnp.int32)
    error = error[0]

    groups = [[e * 4 + f for f in range(4)] for e in range(4)]
    tokens = lax.all_gather(grad_out, "dp", axis_index_groups=groups)

    qt = q_init.T
    q_near = [qt] + [along_x(qt, -d) for d in (1, 2, 3)]
    piece = lax.dynamic_slice_in_dim(weight, z * 1024 + y * 256, 256, 0)
    pieces = [piece, along_x(piece, 1), along_x(after(piece, q_near[1]), 2), along_x(piece, 3)]
    term = error_left(place, qt, error)
    q_far = other_core(jnp.concatenate([qt, after(q_near[1], term, pieces[1], pieces[3]), *q_near[2:]], 0))
    near, far = left(place, q_near, q_far, grad_out, ctx, term)
    half = near + other_core(far)

    passed = other_core(after(cut_far(place, grad_out), near))
    blocks = [half[:8]] + [along_y(half[8 * d : 8 * d + 8], d) for d in (1, 2, 3)]
    blocks[3] = after(blocks[3], pieces[2], passed)
    summed = pair_sum(blocks)
    w0 = after(jnp.stack(pieces), summed)
    w1, w3 = [along_y(w0, d) for d in (-1, 1)]
    summed = pair_sum([summed] + [along_x(summed, d) for d in (1, 2, 3)])
    sends = cut(place, grad_out, after(passed, summed))
    chunk1, chunk3 = [along_x(sends[d], d) for d in (1, 3)]
    over_z = [summed] + [along_z(summed, d) for d in (1, 2, 3)]
    over_z[3] = after(over_z[3], w1, w3, chunk1, chunk3)
    rows = pair_sum(over_z)
    ctx_all = lax.all_gather(after(ctx, rows, tokens), "fsdp", axis=0, tiled=True)
    p_near = [rows] + [along_y(rows, -d) for d in (1, 2, 3)]
    chunk2 = along_x(after(sends[2], rows), 2)
    their1, their3 = [other_core(after(v, rows)) for v in (w1, w3)]
    p_far = other_core(jnp.concatenate([rows, after(p_near[1], their1, their3, chunk2), *p_near[2:]], 0))
    w2 = along_y(after(w0, *p_near), 2)

    turned = turn(place, [sends[0], chunk1, chunk2, chunk3])
    p_raw, u = middle(place, p_near, after(p_far, turned), ctx)
    u_near = [u] + [along_x(u, -d) for d in (1, 2, 3)]
    w_term = right(p_raw, error)
    their0 = other_core(after(w0, u))
    u_far = other_core(jnp.concatenate([u, u_near[1], u_near[2], after(u_near[3], w_term, their0)], 0))
    w = collect(place, w_term, turned, u_near, u_far)
    w = [w] + [along_z(w, d) for d in (1, 2, 3)]
    inverse, p = solve(p_raw)
    w = pair_sum([w[0], w[1], w[2], after(w[3], p, w2)])
    their2 = other_core(after(w2, w))
    w = [w] + [along_y(w, d) for d in (1, 2, 3)]
    outs = share(place, tokens, [w0, w1, w2, w3], [their0, their1, their2, their3])
    w = pair_sum([w[0], w[1], w[2], after(w[3], outs[0])])
    outs = [outs[0]] + [along_z(outs[d], d) for d in (1, 2, 3)]
    q_factor, new_error = last(inverse, w, turned, p, error, ctx_all)
    grad_ctx = join(place, [outs[0], outs[3], outs[2], after(outs[1], q_factor)])
    return (grad_ctx, q_factor.T, new_error[None])


def solution(mesh):
    in_specs = (
        P(("dp", "fsdp"), None),
        P(("dp", "fsdp"), None),
        P(None, "fsdp"),
        P("dp", "fsdp", None),
        P("fsdp", None),
    )
    out_specs = (P(("dp", "fsdp"), None), P("fsdp", None), P("dp", "fsdp", None))
    return jax.shard_map(local, mesh=mesh, in_specs=in_specs, out_specs=out_specs, check_vma=False)
```

```python
import functools

import jax
import jax.numpy as jnp
from jax import lax
from jax.experimental import pallas as pl
from jax.experimental.pallas import tpu as pltpu
from jax.sharding import PartitionSpec as P

F32, BF16 = jnp.float32, jnp.bfloat16
VMEM = pl.BlockSpec(memory_space=pltpu.VMEM)
SMEM = pl.BlockSpec(memory_space=pltpu.SMEM)
HBM = pl.BlockSpec(memory_space=pltpu.HBM)
RELATIVE = [(a, d) for a in range(2) for d in range(4)]
NT = (((1,), (1,)), ((), ()))
NN = (((1,), (0,)), ((), ()))


def mm(lhs, rhs, dims=NN, precision=None):
    return lax.dot_general(lhs, rhs, dims, precision=precision, preferred_element_type=F32)


def halves(value):
    high = value.astype(BF16)
    return high, (value - high.astype(F32)).astype(BF16)


def thirds(value):
    high = value.astype(BF16)
    rest = value - high.astype(F32)
    mid = rest.astype(BF16)
    return high, mid, (rest - mid.astype(F32)).astype(BF16)


def along_x(value, d):
    return lax.ppermute(value, "fsdp", [(i, ((i // 2 + d) % 4) * 2 + i % 2) for i in range(8)])


def along_y(value, d):
    return lax.ppermute(value, "dp", [(i, ((i // 4 + d) % 4) * 4 + i % 4) for i in range(16)])


def along_z(value, d):
    return lax.ppermute(value, "dp", [(i, (i // 4) * 4 + (i % 4 + d) % 4) for i in range(16)])


def other_core(value):
    return lax.ppermute(value, "fsdp", [(i, i ^ 1) for i in range(8)])


def to_relative(value, a, d):
    return lax.ppermute(value, "fsdp", [(i, ((i // 2 + d) % 4) * 2 + (i % 2 ^ a)) for i in range(8)])


def pallas(body, out_shape, mib=16, **kw):
    return pl.pallas_call(
        body,
        out_shape=out_shape,
        compiler_params=pltpu.CompilerParams(vmem_limit_bytes=mib * 2**20),
        cost_estimate=pl.CostEstimate(flops=0, bytes_accessed=0, transcendentals=0),
        **kw,
    )


def in_hbm(value):
    return pltpu.with_memory_space_constraint(value, pltpu.HBM)


def shaped(shape, dtype=F32):
    return jax.ShapeDtypeStruct(shape, dtype)


def after(value, *earlier):
    return lax.optimization_barrier((value, *earlier))[0]


def chunk_of(x, c, a, d):
    return lax.rem(x + d, 4) * 2 + (c ^ a)


def rank_row(y, c, a, d):
    return pl.multiple_of((c ^ a) * 32 + lax.rem(y + d, 4) * 8, 8)


def cut_far_body(place, grad, out):
    for d in range(4):
        out[d] = grad[:, pl.ds(pl.multiple_of(chunk_of(place[0], place[1], 1, d) * 512, 512), 512)]


def cut_far(place, grad):
    return pallas(cut_far_body, shaped((4, 128, 512), BF16), in_specs=[SMEM, VMEM], out_specs=VMEM)(place, grad)


def cut_body(place, grad, passed, *outs):
    for d, out in enumerate(outs):
        out[0] = grad[:, pl.ds(pl.multiple_of(chunk_of(place[0], place[1], 0, d) * 512, 512), 512)]
        out[1] = passed[d]


def cut(place, grad, passed):
    return pallas(cut_body, [shaped((2, 128, 512), BF16)] * 4, in_specs=[SMEM, VMEM, VMEM], out_specs=[VMEM] * 4)(place, grad, passed)


def columns(i):
    return slice(1024 * i, 1024 * i + 1024)


EVEN = [columns(i) for i in range(4)]
ENDS_SMALL = [slice(0, 512), slice(512, 1536), slice(1536, 2560), slice(2560, 3584), slice(3584, 4096)]


class Fetch:
    def __init__(self, source, held, arrived, ahead, parts=EVEN):
        self.copies = [pltpu.make_async_copy(source.at[:, at], held.at[:, at], arrived.at[i]) for i, at in enumerate(parts)]
        self.ahead = ahead
        for copy in self.copies[:ahead]:
            copy.start()

    def wait(self, i):
        if i + self.ahead < len(self.copies):
            self.copies[i + self.ahead].start()
        self.copies[i].wait()


def error_left_body(place, qt, error, out, held, arrived, pieces):
    c, y = place[1], place[2]
    blocks = Fetch(error, held, arrived, 3)
    for n, (a, d) in enumerate(RELATIVE):
        rows = qt[pl.ds(rank_row(y, c, a, d), 8), :]
        high = rows.astype(BF16).astype(F32)
        pieces[8 * n : 8 * n + 8, :] = high
        pieces[64 + 8 * n : 72 + 8 * n, :] = rows - high
    q = pieces[...].astype(BF16)
    for i in range(4):
        blocks.wait(i)
        high, low = halves(held[:, columns(i)])
        first = mm(q, high)
        out[:, columns(i)] = first[:64] + first[64:] + mm(q[:64], low)


def error_left(place, qt, error):
    return pallas(
        error_left_body,
        shaped((64, 4096)),
        in_specs=[SMEM, VMEM, HBM],
        out_specs=VMEM,
        scratch_shapes=[pltpu.VMEM((512, 4096), F32), pltpu.SemaphoreType.DMA((4,)), pltpu.VMEM((128, 512), F32)],
    )(place, qt, in_hbm(error))


def left_body(place, q0, q1, q2, q3, q_far, grad, ctx, term, near, far, g_abs, g_rel):
    x, c, y = place[0], place[1], place[2]
    total = jnp.zeros((64, 128), F32)
    for a, d in RELATIVE:
        q = (q0, q1, q2, q3)[d][...] if a == 0 else q_far[64 * d : 64 * d + 64, :]
        chunk = grad[:, pl.ds(pl.multiple_of(chunk_of(x, c, a, d) * 512, 512), 512)]
        parts = mm(jnp.concatenate(thirds(q), 0), chunk, NT)
        total += parts[:64] + parts[64:128] + parts[128:]
    g_abs[...] = total
    for n, (a, d) in enumerate(RELATIVE):
        g_rel[8 * n : 8 * n + 8, :] = g_abs[pl.ds(rank_row(y, c, a, d), 8), :]
    g = jnp.concatenate(thirds(g_rel[...]), 0)
    for i in range(4):
        at = slice(1024 * i, 1024 * i + 1024)
        parts = mm(g, ctx[:, at])
        whole = term[:, at] + (parts[:64] + parts[64:128] + parts[128:])
        near[:, at] = whole[:32]
        far[:, at] = whole[32:]


def left(place, q_near, q_far, grad, ctx, term):
    return pallas(
        left_body,
        [shaped((32, 4096))] * 2,
        in_specs=[SMEM] + [VMEM] * 8,
        out_specs=[VMEM] * 2,
        scratch_shapes=[pltpu.VMEM((64, 128), F32)] * 2,
    )(place, *q_near, q_far, grad, ctx, term)


def join_body(place, v0, v1, v2, v3, out, done):
    copies = []
    for d, value in enumerate((v0, v1, v2, v3)):
        at = pl.ds(pl.multiple_of(lax.rem(place[3] + d, 4) * 1024, 1024), 1024)
        copies.append(pltpu.make_async_copy(value, out.at[:, at], done.at[d]))
        copies[-1].start()
    for copy in copies:
        copy.wait()


def join(place, values):
    return pallas(
        join_body,
        shaped((128, 4096), BF16),
        in_specs=[SMEM] + [VMEM] * 4,
        out_specs=HBM,
        scratch_shapes=[pltpu.SemaphoreType.DMA((4,))],
    )(place, *values)


def turn_body(place, c0, c1, c2, c3, out, held, done):
    x, c = place[0], place[1]
    copies = [pltpu.make_async_copy(chunk, held.at[d], done.at[d]) for d, chunk in enumerate((c0, c1, c2, c3))]
    for copy in copies:
        copy.start()
    for d, copy in enumerate(copies):
        copy.wait()
        for a in range(2):
            first = pl.multiple_of(chunk_of(x, c, a, 4 - d) * 128, 128)
            out[:, pl.ds(first, 128)] = held[d, a].T


def turn(place, chunks):
    return pallas(
        turn_body,
        shaped((512, 1024), BF16),
        in_specs=[SMEM] + [HBM] * 4,
        out_specs=VMEM,
        scratch_shapes=[pltpu.VMEM((4, 2, 128, 512), BF16), pltpu.SemaphoreType.DMA((4,))],
    )(place, *[in_hbm(chunk) for chunk in chunks])


def middle_body(place, p0, p1, p2, p3, p_far, ctx, p_out, u_out):
    c, y = place[1], place[2]
    for a, d in RELATIVE:
        p_out[pl.ds(rank_row(y, c, a, d), 8), :] = (p0, p1, p2, p3)[d][...] if a == 0 else p_far[8 * d : 8 * d + 8, :]
    u = jnp.zeros((64, 128), F32)
    for i in range(4):
        at = slice(1024 * i, 1024 * i + 1024)
        parts = mm(jnp.concatenate(thirds(p_out[:, at]), 0), ctx[:, at], NT)
        u += parts[:64] + parts[64:128] + parts[128:]
    u_out[...] = u


def middle(place, p_near, p_far, ctx):
    return pallas(
        middle_body,
        [shaped((64, 4096)), shaped((64, 128))],
        in_specs=[SMEM] + [VMEM] * 6,
        out_specs=[VMEM] * 2,
    )(place, *p_near, p_far, ctx)


def right_body(p_raw, error, out, held, arrived):
    blocks = Fetch(error, held, arrived, 3)
    for i in range(4):
        high, low = halves(p_raw[:, columns(i)])
        blocks.wait(i)
        e_high, e_low = halves(held[:, columns(i)])
        parts = mm(e_high, jnp.concatenate([high, low], 0), NT)
        part = parts[:, :64] + parts[:, 64:] + mm(e_low, high, NT)
        if i == 0:
            out[...] = part
        else:
            out[...] += part


def right(p_raw, error):
    return pallas(
        right_body,
        shaped((512, 64)),
        in_specs=[VMEM, HBM],
        out_specs=VMEM,
        scratch_shapes=[pltpu.VMEM((512, 4096), F32), pltpu.SemaphoreType.DMA((4,))],
    )(p_raw, in_hbm(error))


def collect_body(place, term, turned, u0, u1, u2, u3, u_far, out, u_all):
    x, c = place[0], place[1]
    for a, d in RELATIVE:
        u = (u0, u1, u2, u3)[d][...] if a == 0 else u_far[64 * d : 64 * d + 64, :]
        first = pl.multiple_of(chunk_of(x, c, a, d) * 128, 128)
        for n, part in enumerate(thirds(u)):
            u_all[64 * n : 64 * n + 64, pl.ds(first, 128)] = part
    parts = mm(u_all[...], turned[...], NT)
    out[...] = term[...].T + (parts[:64] + parts[64:128] + parts[128:])


def collect(place, term, turned, u_near, u_far):
    return pallas(
        collect_body,
        shaped((64, 512)),
        in_specs=[SMEM] + [VMEM] * 7,
        out_specs=VMEM,
        scratch_shapes=[pltpu.VMEM((192, 1024), BF16)],
    )(place, term, turned, *u_near, u_far)


def solve_body(p_raw, inverse):
    squares = jnp.zeros((192, 192), F32)
    for i in range(4):
        stack = jnp.concatenate(thirds(p_raw[:, 1024 * i : 1024 * i + 1024]), 0)
        squares += mm(stack, stack, NT)
    gram = squares[:64, :64] + (
        (squares[:64, 64:128] + squares[64:128, :64]) + (squares[:64, 128:] + squares[128:, :64] + squares[64:128, 64:128])
    )
    same = lax.broadcasted_iota(jnp.int32, (64, 64), 0) == lax.broadcasted_iota(jnp.int32, (64, 64), 1)
    row = lax.broadcasted_iota(jnp.int32, (64, 128), 0)
    both = jnp.concatenate([gram, jnp.where(same, 1.0, 0.0).astype(F32)], 1)
    for k in range(64):
        scale = both[:, k : k + 1] / both[k : k + 1, k : k + 1]
        both = both - jnp.where(row > k, scale * both[k : k + 1, :], 0.0)
    diagonal = jnp.sum(jnp.where(same, both[:, :64], 0.0), 1, keepdims=True)
    inverse[...] = both[:, 64:] / jnp.sqrt(diagonal)


def solve(p_raw):
    return pallas(solve_body, shaped((64, 64)), in_specs=[VMEM], out_specs=VMEM)(p_raw)


def last_body(inverse, w, turned, p_raw, error, ctx, q_out, out, held, held_ctx, arrived, arrived_ctx, left_here):
    ctx_blocks, blocks = Fetch(ctx, held_ctx, arrived_ctx, 1, ENDS_SMALL), Fetch(error, held, arrived, 1, ENDS_SMALL)
    q = mm(inverse[...], w[...], NN, lax.Precision.HIGHEST) * (1.0 / 16)
    q_out[...] = q
    high, low = halves(q)
    q_split = jnp.concatenate([high, high, low], 0).T
    high, low = halves(inverse[...])
    inverse_split = jnp.concatenate([high, high, low], 1)
    stores = []
    for i, at in enumerate(ENDS_SMALL):
        high, low = halves(p_raw[:, at])
        high, low = halves(mm(inverse_split, jnp.concatenate([high, low, high], 0)))
        approx = mm(q_split, jnp.concatenate([high, low, high], 0))
        ctx_blocks.wait(i)
        product = mm(turned[...], held_ctx[:, at])
        blocks.wait(i)
        held[:, at] = (held[:, at] + product) - approx
        stores.append(pltpu.make_async_copy(held.at[:, at], out.at[:, at], left_here.at[i]))
        stores[-1].start()
    for store in stores:
        store.wait()


def last(inverse, w, turned, p_raw, error, ctx):
    return pallas(
        last_body,
        [shaped((64, 512)), shaped((512, 4096))],
        mib=24,
        in_specs=[VMEM] * 4 + [HBM] * 2,
        out_specs=[VMEM, HBM],
        scratch_shapes=[pltpu.VMEM((512, 4096), F32), pltpu.VMEM((1024, 4096), BF16)] + [pltpu.SemaphoreType.DMA((5,))] * 3,
    )(inverse, w, turned, p_raw, in_hbm(error), in_hbm(ctx))


def share_body(place, tokens, *refs):
    slabs, outs, whole = refs[:8], refs[8:12], refs[12]
    x, c, y, z = place[0], place[1], place[2], place[3]
    for e in range(4):
        total = jnp.zeros((512, 256), F32)
        for a in range(2):
            for d in range(4):
                at = pl.ds(pl.multiple_of(chunk_of(x, c, a, 4 - d) * 512, 512), 512)
                total += mm(tokens[:, :, at].reshape(512, 512), slabs[4 * a + e][d], NT)
        whole[:, pl.ds(pl.multiple_of(lax.rem(y + e, 4) * 256, 256), 256)] = total.astype(BF16)
    for d, out in enumerate(outs):
        out[...] = whole[pl.ds(pl.multiple_of(lax.rem(z + d, 4) * 128, 128), 128), :]


def share(place, tokens, mine, theirs):
    return pallas(
        share_body,
        [shaped((128, 1024), BF16)] * 4,
        mib=24,
        in_specs=[SMEM] + [VMEM] * 9,
        out_specs=[VMEM] * 4,
        scratch_shapes=[pltpu.VMEM((512, 1024), BF16)],
    )(place, tokens, *mine, *theirs)


def pair_sum(values):
    return (values[0] + values[2]) + (values[1] + values[3])


def local(ctx, grad_out, weight, error, q_init):
    j, k = lax.axis_index("fsdp"), lax.axis_index("dp")
    x, c, y, z = j // 2, j % 2, k // 4, k % 4
    place = jnp.stack([x, c, y, z]).astype(jnp.int32)
    error = error[0]

    groups = [[e * 4 + f for f in range(4)] for e in range(4)]
    tokens = lax.all_gather(grad_out, "dp", axis_index_groups=groups)

    qt = q_init.T
    q_near = [qt] + [along_x(qt, -d) for d in (1, 2, 3)]
    piece = lax.dynamic_slice_in_dim(weight, z * 1024 + y * 256, 256, 0)
    pieces = [piece, along_x(piece, 1), along_x(after(piece, q_near[1]), 2), along_x(piece, 3)]
    term = error_left(place, qt, error)
    q_far = other_core(jnp.concatenate([qt, after(q_near[1], term, pieces[1], pieces[3]), *q_near[2:]], 0))
    near, far = left(place, q_near, q_far, grad_out, ctx, term)
    half = near + other_core(far)

    passed = other_core(after(cut_far(place, grad_out), near))
    blocks = [half[:8]] + [along_y(half[8 * d : 8 * d + 8], d) for d in (1, 2, 3)]
    blocks[3] = after(blocks[3], passed)
    summed = pair_sum(blocks)
    w0 = after(jnp.stack(pieces), summed)
    w1, w3 = [along_y(w0, d) for d in (-1, 1)]
    summed = pair_sum([summed] + [along_x(summed, d) for d in (1, 2, 3)])
    sends = cut(place, grad_out, after(passed, summed))
    chunk1, chunk3 = [along_x(sends[d], d) for d in (1, 3)]
    over_z = [summed] + [along_z(summed, d) for d in (1, 2, 3)]
    over_z[3] = after(over_z[3], w1, w3, chunk1, chunk3)
    rows = pair_sum(over_z)
    ctx_all = lax.all_gather(after(ctx, rows, tokens), "fsdp", axis=0, tiled=True)
    p_near = [rows] + [along_y(rows, -d) for d in (1, 2, 3)]
    chunk2 = along_x(after(sends[2], rows), 2)
    their1 = other_core(after(w1, rows))
    p_far = other_core(jnp.concatenate([rows, after(p_near[1], their1, chunk2), *p_near[2:]], 0))
    w2 = along_y(after(w0, *p_near), 2)

    turned = turn(place, [sends[0], chunk1, chunk2, chunk3])
    p_raw, u = middle(place, p_near, after(p_far, turned), ctx)
    u_near = [u] + [along_x(u, -d) for d in (1, 2, 3)]
    w_term = right(p_raw, error)
    their0, their3 = other_core(after(w0, u)), other_core(after(w3, u))
    u_far = other_core(jnp.concatenate([u, u_near[1], u_near[2], after(u_near[3], w_term, their0, their3)], 0))
    w = collect(place, w_term, turned, u_near, u_far)
    w = [w] + [along_z(w, d) for d in (1, 2, 3)]
    inverse = solve(p_raw)
    w = pair_sum([w[0], w[1], w[2], after(w[3], inverse, w2)])
    their2 = other_core(after(w2, w))
    w = [w] + [along_y(w, d) for d in (1, 2, 3)]
    outs = share(place, tokens, [w0, w1, w2, w3], [their0, their1, their2, their3])
    w = pair_sum([w[0], w[1], w[2], after(w[3], outs[0])])
    outs = [outs[0]] + [along_z(outs[d], d) for d in (1, 2, 3)]
    q_factor, new_error = last(inverse, w, turned, p_raw, error, ctx_all)
    grad_ctx = join(place, [outs[0], outs[3], outs[2], after(outs[1], q_factor)])
    return (grad_ctx, q_factor.T, new_error[None])


def solution(mesh):
    in_specs = (
        P(("dp", "fsdp"), None),
        P(("dp", "fsdp"), None),
        P(None, "fsdp"),
        P("dp", "fsdp", None),
        P("fsdp", None),
    )
    out_specs = (P(("dp", "fsdp"), None), P("fsdp", None), P("dp", "fsdp", None))
    return jax.shard_map(local, mesh=mesh, in_specs=in_specs, out_specs=out_specs, check_vma=False)
```

```python
import functools

import jax
import jax.numpy as jnp
from jax import lax
from jax.experimental import pallas as pl
from jax.experimental.pallas import tpu as pltpu
from jax.sharding import PartitionSpec as P

F32, BF16 = jnp.float32, jnp.bfloat16
VMEM = pl.BlockSpec(memory_space=pltpu.VMEM)
SMEM = pl.BlockSpec(memory_space=pltpu.SMEM)
HBM = pl.BlockSpec(memory_space=pltpu.HBM)
RELATIVE = [(a, d) for a in range(2) for d in range(4)]
NT = (((1,), (1,)), ((), ()))
NN = (((1,), (0,)), ((), ()))


def mm(lhs, rhs, dims=NN, precision=None):
    return lax.dot_general(lhs, rhs, dims, precision=precision, preferred_element_type=F32)


def halves(value):
    high = value.astype(BF16)
    return high, (value - high.astype(F32)).astype(BF16)


def thirds(value):
    high = value.astype(BF16)
    rest = value - high.astype(F32)
    mid = rest.astype(BF16)
    return high, mid, (rest - mid.astype(F32)).astype(BF16)


def along_x(value, d):
    return lax.ppermute(value, "fsdp", [(i, ((i // 2 + d) % 4) * 2 + i % 2) for i in range(8)])


def along_y(value, d):
    return lax.ppermute(value, "dp", [(i, ((i // 4 + d) % 4) * 4 + i % 4) for i in range(16)])


def along_z(value, d):
    return lax.ppermute(value, "dp", [(i, (i // 4) * 4 + (i % 4 + d) % 4) for i in range(16)])


def other_core(value):
    return lax.ppermute(value, "fsdp", [(i, i ^ 1) for i in range(8)])


def to_relative(value, a, d):
    return lax.ppermute(value, "fsdp", [(i, ((i // 2 + d) % 4) * 2 + (i % 2 ^ a)) for i in range(8)])


def pallas(body, out_shape, mib=16, **kw):
    return pl.pallas_call(
        body,
        out_shape=out_shape,
        compiler_params=pltpu.CompilerParams(vmem_limit_bytes=mib * 2**20),
        cost_estimate=pl.CostEstimate(flops=0, bytes_accessed=0, transcendentals=0),
        **kw,
    )


def in_hbm(value):
    return pltpu.with_memory_space_constraint(value, pltpu.HBM)


def shaped(shape, dtype=F32):
    return jax.ShapeDtypeStruct(shape, dtype)


def after(value, *earlier):
    return lax.optimization_barrier((value, *earlier))[0]


def chunk_of(x, c, a, d):
    return lax.rem(x + d, 4) * 2 + (c ^ a)


def rank_row(y, c, a, d):
    return pl.multiple_of((c ^ a) * 32 + lax.rem(y + d, 4) * 8, 8)


def cut_far_body(place, grad, out):
    for d in range(4):
        out[d] = grad[:, pl.ds(pl.multiple_of(chunk_of(place[0], place[1], 1, d) * 512, 512), 512)]


def cut_far(place, grad):
    return pallas(cut_far_body, shaped((4, 128, 512), BF16), in_specs=[SMEM, VMEM], out_specs=VMEM)(place, grad)


def cut_body(place, grad, passed, *outs):
    for d, out in enumerate(outs):
        out[0] = grad[:, pl.ds(pl.multiple_of(chunk_of(place[0], place[1], 0, d) * 512, 512), 512)]
        out[1] = passed[d]


def cut(place, grad, passed):
    return pallas(cut_body, [shaped((2, 128, 512), BF16)] * 4, in_specs=[SMEM, VMEM, VMEM], out_specs=[VMEM] * 4)(place, grad, passed)


def columns(i):
    return slice(1024 * i, 1024 * i + 1024)


EVEN = [columns(i) for i in range(4)]
ENDS_SMALL = [slice(0, 512), slice(512, 1536), slice(1536, 2560), slice(2560, 3584), slice(3584, 4096)]


class Fetch:
    def __init__(self, source, held, arrived, ahead, parts=EVEN):
        self.copies = [pltpu.make_async_copy(source.at[:, at], held.at[:, at], arrived.at[i]) for i, at in enumerate(parts)]
        self.ahead = ahead
        for copy in self.copies[:ahead]:
            copy.start()

    def wait(self, i):
        if i + self.ahead < len(self.copies):
            self.copies[i + self.ahead].start()
        self.copies[i].wait()


def error_left_body(place, qt, error, out, held, arrived, pieces):
    c, y = place[1], place[2]
    blocks = Fetch(error, held, arrived, 3)
    for n, (a, d) in enumerate(RELATIVE):
        rows = qt[pl.ds(rank_row(y, c, a, d), 8), :]
        high = rows.astype(BF16).astype(F32)
        pieces[8 * n : 8 * n + 8, :] = high
        pieces[64 + 8 * n : 72 + 8 * n, :] = rows - high
    q = pieces[...].astype(BF16)
    for i in range(4):
        blocks.wait(i)
        high, low = halves(held[:, columns(i)])
        first = mm(q, high)
        out[:, columns(i)] = first[:64] + first[64:] + mm(q[:64], low)


def error_left(place, qt, error):
    return pallas(
        error_left_body,
        shaped((64, 4096)),
        in_specs=[SMEM, VMEM, HBM],
        out_specs=VMEM,
        scratch_shapes=[pltpu.VMEM((512, 4096), F32), pltpu.SemaphoreType.DMA((4,)), pltpu.VMEM((128, 512), F32)],
    )(place, qt, in_hbm(error))


def left_body(place, q0, q1, q2, q3, q_far, grad, ctx, term, near, far, g_abs, g_rel):
    x, c, y = place[0], place[1], place[2]
    total = jnp.zeros((64, 128), F32)
    for a, d in RELATIVE:
        q = (q0, q1, q2, q3)[d][...] if a == 0 else q_far[64 * d : 64 * d + 64, :]
        chunk = grad[:, pl.ds(pl.multiple_of(chunk_of(x, c, a, d) * 512, 512), 512)]
        parts = mm(jnp.concatenate(thirds(q), 0), chunk, NT)
        total += parts[:64] + parts[64:128] + parts[128:]
    g_abs[...] = total
    for n, (a, d) in enumerate(RELATIVE):
        g_rel[8 * n : 8 * n + 8, :] = g_abs[pl.ds(rank_row(y, c, a, d), 8), :]
    g = jnp.concatenate(thirds(g_rel[...]), 0)
    for i in range(4):
        at = slice(1024 * i, 1024 * i + 1024)
        parts = mm(g, ctx[:, at])
        whole = term[:, at] + (parts[:64] + parts[64:128] + parts[128:])
        near[:, at] = whole[:32]
        far[:, at] = whole[32:]


def left(place, q_near, q_far, grad, ctx, term):
    return pallas(
        left_body,
        [shaped((32, 4096))] * 2,
        in_specs=[SMEM] + [VMEM] * 8,
        out_specs=[VMEM] * 2,
        scratch_shapes=[pltpu.VMEM((64, 128), F32)] * 2,
    )(place, *q_near, q_far, grad, ctx, term)


def join_body(place, v0, v1, v2, v3, out, done):
    copies = []
    for d, value in enumerate((v0, v1, v2, v3)):
        at = pl.ds(pl.multiple_of(lax.rem(place[3] + d, 4) * 1024, 1024), 1024)
        copies.append(pltpu.make_async_copy(value, out.at[:, at], done.at[d]))
        copies[-1].start()
    for copy in copies:
        copy.wait()


def join(place, values):
    return pallas(
        join_body,
        shaped((128, 4096), BF16),
        in_specs=[SMEM] + [VMEM] * 4,
        out_specs=HBM,
        scratch_shapes=[pltpu.SemaphoreType.DMA((4,))],
    )(place, *values)


def turn_body(place, c0, c1, c2, c3, out, held, done):
    x, c = place[0], place[1]
    copies = [pltpu.make_async_copy(chunk, held.at[d], done.at[d]) for d, chunk in enumerate((c0, c1, c2, c3))]
    for copy in copies:
        copy.start()
    for d, copy in enumerate(copies):
        copy.wait()
        for a in range(2):
            first = pl.multiple_of(chunk_of(x, c, a, 4 - d) * 128, 128)
            out[:, pl.ds(first, 128)] = held[d, a].T


def turn(place, chunks):
    return pallas(
        turn_body,
        shaped((512, 1024), BF16),
        in_specs=[SMEM] + [HBM] * 4,
        out_specs=VMEM,
        scratch_shapes=[pltpu.VMEM((4, 2, 128, 512), BF16), pltpu.SemaphoreType.DMA((4,))],
    )(place, *[in_hbm(chunk) for chunk in chunks])


def middle_body(place, p0, p1, p2, p3, p_far, ctx, p_out, u_out):
    c, y = place[1], place[2]
    for a, d in RELATIVE:
        p_out[pl.ds(rank_row(y, c, a, d), 8), :] = (p0, p1, p2, p3)[d][...] if a == 0 else p_far[8 * d : 8 * d + 8, :]
    u = jnp.zeros((64, 128), F32)
    for i in range(4):
        at = slice(1024 * i, 1024 * i + 1024)
        parts = mm(jnp.concatenate(thirds(p_out[:, at]), 0), ctx[:, at], NT)
        u += parts[:64] + parts[64:128] + parts[128:]
    u_out[...] = u


def middle(place, p_near, p_far, ctx):
    return pallas(
        middle_body,
        [shaped((64, 4096)), shaped((64, 128))],
        in_specs=[SMEM] + [VMEM] * 6,
        out_specs=[VMEM] * 2,
    )(place, *p_near, p_far, ctx)


def right_body(p_raw, error, out, held, arrived):
    blocks = Fetch(error, held, arrived, 3)
    for i in range(4):
        high, low = halves(p_raw[:, columns(i)])
        blocks.wait(i)
        e_high, e_low = halves(held[:, columns(i)])
        parts = mm(e_high, jnp.concatenate([high, low], 0), NT)
        part = parts[:, :64] + parts[:, 64:] + mm(e_low, high, NT)
        if i == 0:
            out[...] = part
        else:
            out[...] += part


def right(p_raw, error):
    return pallas(
        right_body,
        shaped((512, 64)),
        in_specs=[VMEM, HBM],
        out_specs=VMEM,
        scratch_shapes=[pltpu.VMEM((512, 4096), F32), pltpu.SemaphoreType.DMA((4,))],
    )(p_raw, in_hbm(error))


def collect_body(place, term, turned, u0, u1, u2, u3, u_far, out, u_all):
    x, c = place[0], place[1]
    for a, d in RELATIVE:
        u = (u0, u1, u2, u3)[d][...] if a == 0 else u_far[64 * d : 64 * d + 64, :]
        first = pl.multiple_of(chunk_of(x, c, a, d) * 128, 128)
        for n, part in enumerate(thirds(u)):
            u_all[64 * n : 64 * n + 64, pl.ds(first, 128)] = part
    parts = mm(u_all[...], turned[...], NT)
    out[...] = term[...].T + (parts[:64] + parts[64:128] + parts[128:])


def collect(place, term, turned, u_near, u_far):
    return pallas(
        collect_body,
        shaped((64, 512)),
        in_specs=[SMEM] + [VMEM] * 7,
        out_specs=VMEM,
        scratch_shapes=[pltpu.VMEM((192, 1024), BF16)],
    )(place, term, turned, *u_near, u_far)


def solve_body(p_raw, inverse):
    squares = jnp.zeros((192, 192), F32)
    for i in range(4):
        stack = jnp.concatenate(thirds(p_raw[:, 1024 * i : 1024 * i + 1024]), 0)
        squares += mm(stack, stack, NT)
    gram = squares[:64, :64] + (
        (squares[:64, 64:128] + squares[64:128, :64]) + (squares[:64, 128:] + squares[128:, :64] + squares[64:128, 64:128])
    )
    same = lax.broadcasted_iota(jnp.int32, (64, 64), 0) == lax.broadcasted_iota(jnp.int32, (64, 64), 1)
    row = lax.broadcasted_iota(jnp.int32, (64, 128), 0)
    both = jnp.concatenate([gram, jnp.where(same, 1.0, 0.0).astype(F32)], 1)
    for k in range(64):
        scale = both[:, k : k + 1] / both[k : k + 1, k : k + 1]
        both = both - jnp.where(row > k, scale * both[k : k + 1, :], 0.0)
    diagonal = jnp.sum(jnp.where(same, both[:, :64], 0.0), 1, keepdims=True)
    inverse[...] = both[:, 64:] / jnp.sqrt(diagonal)


def solve(p_raw):
    return pallas(solve_body, shaped((64, 64)), in_specs=[VMEM], out_specs=VMEM)(p_raw)


def last_body(inverse, w, turned, p_raw, error, ctx, q_out, out, held, held_ctx, arrived, arrived_ctx, left_here):
    ctx_blocks, blocks = Fetch(ctx, held_ctx, arrived_ctx, 1, ENDS_SMALL), Fetch(error, held, arrived, 1, ENDS_SMALL)
    q = mm(inverse[...], w[...], NN, lax.Precision.HIGHEST) * (1.0 / 16)
    q_out[...] = q
    high, low = halves(q)
    q_split = jnp.concatenate([high, high, low], 0).T
    high, low = halves(inverse[...])
    inverse_split = jnp.concatenate([high, high, low], 1)
    stores = []
    for i, at in enumerate(ENDS_SMALL):
        high, low = halves(p_raw[:, at])
        high, low = halves(mm(inverse_split, jnp.concatenate([high, low, high], 0)))
        approx = mm(q_split, jnp.concatenate([high, low, high], 0))
        ctx_blocks.wait(i)
        product = mm(turned[...], held_ctx[:, at])
        blocks.wait(i)
        held[:, at] = (held[:, at] + product) - approx
        stores.append(pltpu.make_async_copy(held.at[:, at], out.at[:, at], left_here.at[i]))
        stores[-1].start()
    for store in stores:
        store.wait()


def last(inverse, w, turned, p_raw, error, ctx):
    return pallas(
        last_body,
        [shaped((64, 512)), shaped((512, 4096))],
        mib=24,
        in_specs=[VMEM] * 4 + [HBM] * 2,
        out_specs=[VMEM, HBM],
        scratch_shapes=[pltpu.VMEM((512, 4096), F32), pltpu.VMEM((1024, 4096), BF16)] + [pltpu.SemaphoreType.DMA((5,))] * 3,
    )(inverse, w, turned, p_raw, in_hbm(error), in_hbm(ctx))


def share_body(place, tokens, *refs):
    slabs, outs, whole = refs[:8], refs[8:12], refs[12]
    x, c, y, z = place[0], place[1], place[2], place[3]
    for e in range(4):
        total = jnp.zeros((512, 256), F32)
        for a in range(2):
            for d in range(4):
                at = pl.ds(pl.multiple_of(chunk_of(x, c, a, 4 - d) * 512, 512), 512)
                total += mm(tokens[:, :, at].reshape(512, 512), slabs[4 * a + e][d], NT)
        whole[:, pl.ds(pl.multiple_of(lax.rem(y + e, 4) * 256, 256), 256)] = total.astype(BF16)
    for d, out in enumerate(outs):
        out[...] = whole[pl.ds(pl.multiple_of(lax.rem(z + d, 4) * 128, 128), 128), :]


def share(place, tokens, mine, theirs):
    return pallas(
        share_body,
        [shaped((128, 1024), BF16)] * 4,
        mib=24,
        in_specs=[SMEM] + [VMEM] * 9,
        out_specs=[VMEM] * 4,
        scratch_shapes=[pltpu.VMEM((512, 1024), BF16)],
    )(place, tokens, *mine, *theirs)


def pair_sum(values):
    return (values[0] + values[2]) + (values[1] + values[3])


def local(ctx, grad_out, weight, error, q_init):
    j, k = lax.axis_index("fsdp"), lax.axis_index("dp")
    x, c, y, z = j // 2, j % 2, k // 4, k % 4
    place = jnp.stack([x, c, y, z]).astype(jnp.int32)
    error = error[0]

    groups = [[e * 4 + f for f in range(4)] for e in range(4)]
    tokens = lax.all_gather(grad_out, "dp", axis_index_groups=groups)

    qt = q_init.T
    q_near = [qt] + [along_x(qt, -d) for d in (1, 2, 3)]
    piece = lax.dynamic_slice_in_dim(weight, z * 1024 + y * 256, 256, 0)
    pieces = [piece, along_x(piece, 1), along_x(after(piece, q_near[1]), 2), along_x(piece, 3)]
    term = error_left(place, qt, error)
    q_far = other_core(jnp.concatenate([qt, after(q_near[1], term, pieces[1], pieces[3]), *q_near[2:]], 0))
    near, far = left(place, q_near, q_far, grad_out, ctx, term)
    half = near + other_core(far)

    passed = other_core(after(cut_far(place, grad_out), near))
    blocks = [half[:8]] + [along_y(half[8 * d : 8 * d + 8], d) for d in (1, 2, 3)]
    blocks[3] = after(blocks[3], passed)
    summed = pair_sum(blocks)
    w0 = after(jnp.stack(pieces), summed)
    w1, w3 = [along_y(w0, d) for d in (-1, 1)]
    summed = pair_sum([summed] + [along_x(summed, d) for d in (1, 2, 3)])
    sends = cut(place, grad_out, after(passed, summed))
    chunk1, chunk3 = [along_x(sends[d], d) for d in (1, 3)]
    over_z = [summed] + [along_z(summed, d) for d in (1, 2, 3)]
    over_z[3] = after(over_z[3], w1, w3, chunk1, chunk3)
    rows = pair_sum(over_z)
    ctx_all = lax.all_gather(after(ctx, rows, tokens), "fsdp", axis=0, tiled=True)
    p_near = [rows] + [along_y(rows, -d) for d in (1, 2, 3)]
    chunk2 = along_x(after(sends[2], rows), 2)
    their1 = other_core(after(w1, rows))
    p_far = other_core(jnp.concatenate([rows, after(p_near[1], their1, chunk2), *p_near[2:]], 0))
    w2 = along_y(after(w0, *p_near), 2)

    turned = turn(place, [sends[0], chunk1, chunk2, chunk3])
    p_raw, u = middle(place, p_near, after(p_far, turned), ctx)
    u_near = [u] + [along_x(u, -d) for d in (1, 2, 3)]
    w_term = right(p_raw, error)
    their0 = other_core(after(w0, u))
    u_far = other_core(jnp.concatenate([u, u_near[1], u_near[2], after(u_near[3], w_term, their0)], 0))
    w = collect(place, w_term, turned, u_near, u_far)
    w = [w] + [along_z(w, d) for d in (1, 2, 3)]
    inverse = solve(p_raw)
    w = pair_sum([w[0], w[1], w[2], after(w[3], inverse, w2)])
    their2, their3 = [other_core(after(v, w)) for v in (w2, w3)]
    w = [w] + [along_y(w, d) for d in (1, 2, 3)]
    outs = share(place, tokens, [w0, w1, w2, w3], [their0, their1, their2, their3])
    w = pair_sum([w[0], w[1], w[2], after(w[3], outs[0])])
    outs = [outs[0]] + [along_z(outs[d], d) for d in (1, 2, 3)]
    q_factor, new_error = last(inverse, w, turned, p_raw, error, ctx_all)
    grad_ctx = join(place, [outs[0], outs[3], outs[2], after(outs[1], q_factor)])
    return (grad_ctx, q_factor.T, new_error[None])


def solution(mesh):
    in_specs = (
        P(("dp", "fsdp"), None),
        P(("dp", "fsdp"), None),
        P(None, "fsdp"),
        P("dp", "fsdp", None),
        P("fsdp", None),
    )
    out_specs = (P(("dp", "fsdp"), None), P("fsdp", None), P("dp", "fsdp", None))
    return jax.shard_map(local, mesh=mesh, in_specs=in_specs, out_specs=out_specs, check_vma=False)
```
